32 devices in a mesh: dp: 4 (over y, x), seq: 2 (over core), tensor: 4 (over z).
Axes of the slice: x: 2, y: 2, z: 4, core: 2. Of those that a mesh axis runs over, the one named last changes fastest.
Arguments:
- features: bfloat16 [1024, 4096], P(('dp', 'seq'), 'tensor'), parts along dimension 0, may hold values from -6 to 6
- in_weight: bfloat16 [4096, 3, 4096], P('seq', None, 'tensor'), may hold values from -0.09375 to 0.09375
- short_taps: float32 [3, 7, 4096], P(None, None, 'tensor'), may hold values from -2.5 to 2.5
- decay_rates: float32 [16, 4096], P(None, 'tensor'), may hold values from 0.001953125 to 0.1
- residues: float32 [16, 4096], P(None, 'tensor'), may hold values from -1.5 to 1.5
- skip_gain: float32 [4096], P('tensor'), may hold values from 0.5 to 1.5
- out_weight: bfloat16 [4096, 4096], P(None, 'tensor'), may hold values from -0.09375 to 0.09375
Outputs:
- mixed: bfloat16 [1024, 4096], P(('dp', 'seq'), 'tensor'), parts along dimension 0
The draws below stay inside these ranges and needn't reach their ends.
There are 4 independent parts, one for each index of `dp`. The reference program is written for one: setup_inputs(seed, part) draws one part's arguments, and reference() takes and returns one part's arrays. A program takes and returns all parts, laid end to end along the dimension named above; an argument that names none is the same for every part. Nothing has to cross between parts.
All inputs are finite; a program needn't handle non-finite values.
Results may differ from the reference program's by a relative error of at most 0.007.
Values may be sent and summed in bfloat16 or wider, within the bound.
A program may use at most 128 MiB of HBM per device.

```python
import math
import jax
import jax.numpy as jnp

D = 4096
KS = 7
M = 16
L = 256


def block_levels(own_key, shape, split, smallest, top_value):
    def one(dim, blocks):
        steps = jax.random.uniform(jax.random.fold_in(jax.random.fold_in(own_key, 6), dim), (blocks,), jnp.float32, smallest / len(split), top_value / len(split))
        return jnp.repeat(jnp.exp(steps), shape[dim] // blocks).reshape((-1,) + (1,) * (len(shape) - dim - 1))

    loudness = one(*split[0])
    for cut in split[1:]:
        loudness = loudness * one(*cut)
    return loudness


def noise(stream_key, dims, deviation, reach, pieces=(), kind=jnp.bfloat16):
    drawn = jax.random.normal(stream_key, dims, jnp.float32) * deviation
    if len(pieces) > 0:
        drawn = block_levels(stream_key, dims, pieces, -0.22, 0.18) * drawn
    return jnp.clip(drawn, min=-reach, max=reach).astype(kind)


def setup_inputs(seed: int = 0, part: int = 0) -> dict:
    key_of = jax.random.split(jax.random.key(seed), 8)
    own_keys = jax.random.split(jax.random.fold_in(key_of[7], part), 8)
    features = noise(own_keys[0], (L, D), 1.0, 6.0, ((0, 2), (1, 4)))
    in_weight = noise(key_of[1], (D, 3, D), D ** -0.5, 0.09375, ((0, 2), (2, 4)))
    short_taps = noise(key_of[2], (3, KS, D), 0.4, 2.5, ((2, 4),), jnp.float32)
    decay_rates = jnp.clip(jnp.exp(math.log(0.1) - 3.9357395 * jax.random.uniform(key_of[3], (M, D), jnp.float32) ** block_levels(key_of[3], (M, D), ((1, 4),), -0.2, 0.2)), 0.001953125, 0.1)
    residues = noise(key_of[4], (M, D), M ** -0.5, 1.5, ((1, 4),), jnp.float32)
    skip_gain = jnp.clip(0.5 + 1.0 * jax.random.uniform(key_of[5], (D,), jnp.float32) ** block_levels(key_of[5], (D,), ((0, 4),), -0.2, 0.2), 0.5, 1.5)
    out_weight = noise(key_of[6], (D, D), D ** -0.5, 0.09375, ((1, 4),))
    return {"features": features, "in_weight": in_weight, "short_taps": short_taps, "decay_rates": decay_rates, "residues": residues, "skip_gain": skip_gain, "out_weight": out_weight}


def reference(features, in_weight, short_taps, decay_rates, residues, skip_gain, out_weight):
    length = features.shape[0]
    width = features.shape[1]
    projected = jnp.dot(features, in_weight.reshape(width, 3 * width), preferred_element_type=jnp.float32)
    projected = projected.astype(jnp.bfloat16).reshape(length, 3, width)
    taps_count = short_taps.shape[1]
    rim_rows = taps_count - 1
    extended = jnp.concatenate([jnp.zeros((rim_rows, 3, width), jnp.bfloat16), projected], axis=0).astype(jnp.float32)
    short = jnp.zeros((length, 3, width), jnp.float32)
    for offset_lag in range(taps_count):
        short = short + short_taps[:, offset_lag, :][None] * extended[rim_rows - offset_lag:rim_rows - offset_lag + length]
    product = short[:, 1, :] * short[:, 2, :]
    amplitude = residues * jnp.sqrt(2.0 * decay_rates)
    moments = jnp.arange(length).astype(jnp.float32)
    kernel = jnp.zeros((length, width), jnp.float32)
    for mode_index in range(decay_rates.shape[0]):
        kernel = kernel + amplitude[mode_index][None, :] * jnp.exp(-decay_rates[mode_index][None, :] * moments[:, None])
    padded_len = 2 * length
    spectrum = jnp.fft.rfft(product, padded_len, axis=0) * jnp.fft.rfft(kernel, padded_len, axis=0)
    conv = jnp.fft.irfft(spectrum, padded_len, axis=0)[:length]
    gated = (short[:, 0, :] * (conv + skip_gain[None, :] * product)).astype(jnp.bfloat16)
    return jnp.dot(gated, out_weight, preferred_element_type=jnp.float32).astype(jnp.bfloat16)
```

```python
import functools

import jax
import jax.numpy as jnp
from jax import lax
from jax.experimental import pallas as pl
from jax.experimental.pallas import tpu as pltpu
from jax.sharding import PartitionSpec as P

MESH = pl.DeviceIdType.MESH

precise = lax.Precision.HIGHEST
block_len = 64


def passed_along(value, axis, steps):
    count = lax.axis_size(axis)
    leading, last = (max(0, -steps), min(count, count - steps))
    return lax.ppermute(value, axis, [(source, source + steps) for source in range(leading, last)])


def prefix_2(part, axis, combine, identity):
    place = lax.axis_index(axis)
    gathered = jax.tree.map(lambda a: lax.all_gather(a, axis), part)
    state = jax.tree.map(lambda a, e: jnp.zeros_like(a) + jnp.asarray(e, a.dtype), part, identity)

    def one(turn, state):
        return combine(
            state, jax.tree.map(lambda a: lax.dynamic_index_in_dim(a, turn, 0, False), gathered)
        )

    return lax.fori_loop(0, place, one, state)


def body(features, in_weight, short_taps, decay_rates, residues, skip_gain, out_weight):
    tok_rows = features.shape[0]
    channels = in_weight.shape[2]
    taps_count = short_taps.shape[1]
    whole_feats = lax.all_gather(features, "tensor", axis=1, tiled=True)
    piece = lax.all_gather(in_weight, "seq", axis=0, tiled=True)
    count = piece.shape[0]
    projected = jnp.dot(
        whole_feats, piece.reshape(count, 3 * channels), preferred_element_type=jnp.float32
    )
    projected = projected.astype(jnp.bfloat16).reshape(tok_rows, 3, channels)
    rim_rows = taps_count - 1
    earlier = passed_along(projected[tok_rows - rim_rows :], "seq", 1)
    extended = jnp.concatenate([earlier, projected], axis=0).astype(jnp.float32)
    short = jnp.zeros((tok_rows, 3, channels), jnp.float32)
    for offset_lag in range(taps_count):
        short = (
            short
            + short_taps[:, offset_lag, :][None]
            * extended[rim_rows - offset_lag : rim_rows - offset_lag + tok_rows]
        )
    product = short[:, 1, :] * short[:, 2, :]
    blocks = tok_rows // block_len
    pieces = product.reshape(blocks, block_len, channels)
    amplitude = residues * jnp.sqrt(2.0 * decay_rates)
    offsets = jnp.arange(block_len).astype(jnp.float32)
    falloff = jnp.exp(-decay_rates[:, None, :] * offsets[None, :, None])
    kernel = jnp.einsum("mc,mtc->tc", amplitude, falloff, precision=precise)
    lag_grid = jnp.arange(block_len)[:, None] - jnp.arange(block_len)[None, :]
    select = (lag_grid[:, :, None] == jnp.arange(block_len)[None, None, :]).astype(jnp.float32)
    toeplitz = jnp.einsum("tsk,kc->tsc", select, kernel, precision=precise)
    inner = jnp.einsum("tsc,bsc->btc", toeplitz, pieces, precision=precise)
    toward_end = jnp.exp(-decay_rates[:, None, :] * (block_len - offsets)[None, :, None])
    block_sums = jnp.einsum("msc,bsc->bmc", toward_end, pieces, precision=precise)
    block_index = jnp.arange(blocks).astype(jnp.float32)
    carry_over = jnp.exp(
        -decay_rates[None] * (block_len * (blocks - 1 - block_index))[:, None, None]
    )
    device_sum = jnp.sum(carry_over * block_sums, axis=0)
    device_decay = jnp.exp(-decay_rates * float(tok_rows))

    def combine(earlier_pair, later_pair):
        return (earlier_pair[0] * later_pair[0], later_pair[0] * earlier_pair[1] + later_pair[1])

    prefix = prefix_2(
        (device_decay, device_sum),
        "seq",
        combine,
        (jnp.ones_like(device_decay), jnp.zeros_like(device_sum)),
    )
    entering = prefix[1]
    step_decay = jnp.exp(-decay_rates * float(block_len))

    def advance(state, block_sum):
        return (step_decay * state + block_sum, state)

    final_state, starts = lax.scan(advance, entering, block_sums)
    outer = jnp.einsum("mic,bmc->bic", amplitude[:, None, :] * falloff, starts, precision=precise)
    conv = (inner + outer).reshape(tok_rows, channels)
    gated = (short[:, 0, :] * (conv + skip_gain[None, :] * product)).astype(jnp.bfloat16)
    mixed = jnp.dot(
        lax.all_gather(gated, "tensor", axis=1, tiled=True),
        out_weight,
        preferred_element_type=jnp.float32,
    )
    return mixed.astype(jnp.bfloat16)


def nearest_first(place, step):
    table = ((0, 1, 2, 3), (1, 0, 2, 3), (2, 3, 1, 0), (3, 2, 1, 0))
    found = jnp.int32(table[0][step])
    for at in range(1, 4):
        found = jnp.where(place == at, jnp.int32(table[at][step]), found)
    return found


def fused_kernel(
    feat, w_hbm, taps, decay, resid, skip, ow_hbm, out,
    f, w, ow, psend, precv, own, proj, prod, gate, gbuf, gsend, gath, acc,
    f_send, f_recv, w_sem, ow_sem, p_send, p_recv, g_send, g_recv,
):
    rows, deep = feat.shape
    half = own.shape[-1] * 4
    tile = half // 2
    lanes = own.shape[-1]
    span = 2 * rows // 8
    modes = decay.shape[0]
    taps_count = taps.shape[1]
    rim = taps_count - 1
    s = lax.axis_index("seq")
    t = lax.axis_index("tensor")
    me = t * 2 + s
    others = [(ds, dt) for dt in range(4) for ds in range(2) if (ds, dt) != (0, 0)]

    def device(ds, dt):
        return {"seq": lax.rem(s + ds, 2), "tensor": lax.rem(t + dt, 4)}

    near = jnp.where(t > 2 * s, 1, 0)

    def w_copy(step, j):
        r = near if step == 0 else 1 - near
        rng = pl.ds(pl.multiple_of(r * deep, deep), deep)
        return pltpu.make_async_copy(w_hbm.at[j, rng], w.at[j, rng], w_sem.at[step, j])

    def ow_copy(k):
        rng = pl.ds(k * deep, deep)
        return pltpu.make_async_copy(ow_hbm.at[rng], ow.at[rng], ow_sem.at[k])

    for step in range(2):
        for j in range(3):
            w_copy(step, j).start()

    barrier = pltpu.get_barrier_semaphore()
    for ds, dt in others:
        pl.semaphore_signal(barrier, inc=1, device_id=device(ds, dt), device_id_type=MESH)
    pl.semaphore_wait(barrier, len(others))

    home = t // 2
    slot = lax.rem(t, 2)
    place = pl.ds(pl.multiple_of(s * rows, rows), rows)

    def f_push(dt):
        return pltpu.make_async_remote_copy(
            src_ref=feat,
            dst_ref=f.at[slot, place],
            send_sem=f_send.at[dt],
            recv_sem=f_recv.at[slot, s],
            device_id={"seq": home, "tensor": lax.rem(t + dt, 4)},
            device_id_type=MESH,
        )

    def f_own():
        return pltpu.make_async_copy(feat, f.at[slot, place], f_recv.at[slot, s])

    for dt in (2, 3, 1):
        f_push(dt).start()

    @pl.when(home == s)
    def _():
        f_own().start()

    @pl.when(home != s)
    def _():
        f_push(0).start()

    for k in range(4):
        ow_copy(k).start()

    def p_push(ct, j):
        return pltpu.make_async_remote_copy(
            src_ref=psend.at[ct, j],
            dst_ref=precv.at[ct, j],
            send_sem=p_send.at[ct, j],
            recv_sem=p_recv.at[ct, j],
            device_id=device(1, 0),
            device_id_type=MESH,
        )

    for step in range(2):
        r = near if step == 0 else 1 - near
        for h in range(2):
            part = f.at[r, pl.ds(h * rows, rows)]
            pltpu.make_async_copy(part, part, f_recv.at[r, h]).wait()
        for j in range(3):
            w_copy(step, j).wait()
        depth = pl.ds(pl.multiple_of(r * deep, deep), deep)
        for side in range(2):
            target = psend if side == 0 else own
            base = ((1 - s) if side == 0 else s) * half

            @pl.loop(0, 6)
            def _(idx, target=target, base=base, side=side, step=step, r=r, depth=depth):
                ct, j = idx // 3, lax.rem(idx, 3)
                columns = pl.ds(pl.multiple_of(base + ct * tile, tile), tile)
                part = jnp.dot(f[r], w[j, depth, columns], preferred_element_type=jnp.float32)
                for gl in range(2):
                    piece = part[:, gl * lanes : (gl + 1) * lanes]
                    if step == 0:
                        target[ct, j, gl] = piece
                    else:
                        target[ct, j, gl] += piece
                if step == 1 and side == 0:
                    p_push(ct, j).start()

    first = lax.broadcasted_iota(jnp.int32, (8, lanes), 0)

    def later(value, by):
        return jnp.where(first >= by, pltpu.roll(value, by, 0), 0.0)

    def g_push(n, ct):
        ds, dt = others[n]
        to = lax.rem(s + ds, 2)
        return pltpu.make_async_remote_copy(
            src_ref=gsend.at[ct, pl.ds(pl.multiple_of(to * rows, rows), rows)],
            dst_ref=gath.at[me, :, pl.ds(pl.multiple_of(ct * tile, tile), tile)],
            send_sem=g_send.at[n, ct],
            recv_sem=g_recv.at[me, ct],
            device_id=device(ds, dt),
            device_id_type=MESH,
        )

    @pl.loop(0, 2)
    def _(ct):
        for j in range(3):
            part = precv.at[ct, j]
            pltpu.make_async_copy(part, part, p_recv.at[ct, j]).wait()

        for gl in range(2):
            columns = pl.ds(pl.multiple_of(s * half + ct * tile + gl * lanes, lanes), lanes)

            @pl.loop(0, span)
            def _(i, gl=gl):
                at = pl.ds(i, 8, stride=span)
                for j in range(3):
                    value = own.at[ct, j, gl][at, :] + precv.at[ct, j, gl][at, :]
                    proj[j, rim + i] = value.astype(jnp.bfloat16).astype(jnp.float32)

            for j in range(3):
                for k in range(rim):
                    proj[j, k] = later(proj[j, span + k], 1)

            tap = [
                [jnp.broadcast_to(taps[j, k : k + 1, columns], (8, lanes)) for k in range(taps_count)]
                for j in range(3)
            ]
            rate = [jnp.broadcast_to(decay[m : m + 1, columns], (8, lanes)) for m in range(modes)]

            @pl.loop(0, span, unroll=2)
            def _(i, tap=tap):
                short = []
                for j in range(3):
                    total = tap[j][0] * proj[j, rim + i]
                    for k in range(1, taps_count):
                        total = total + tap[j][k] * proj[j, rim + i - k]
                    short.append(total)
                gate[i] = short[0]
                prod[i] = short[1] * short[2]

            fall = [jnp.exp(-v) for v in rate]

            def gather_state(i, state, fall=fall):
                x = prod[i]
                return tuple(a * v + x for a, v in zip(fall, state))

            zero = jnp.zeros((8, lanes), jnp.float32)
            state = lax.fori_loop(0, span, gather_state, (zero,) * modes, unroll=4)
            start = []
            for m in range(modes):
                jump = jnp.exp(-rate[m] * float(span))
                value = later(state[m], 1)
                for by in (1, 2, 4):
                    value = value + jump * later(value, by)
                    jump = jump * jump
                start.append(value)
            scale = [
                jnp.broadcast_to(resid[m : m + 1, columns], (8, lanes)) * jnp.sqrt(2.0 * rate[m])
                for m in range(modes)
            ]
            direct = jnp.broadcast_to(skip[:, columns], (8, lanes))

            def emit(i, state, fall=fall, scale=scale, direct=direct):
                x = prod[i]
                state = tuple(a * v + x for a, v in zip(fall, state))
                terms = [a * v for a, v in zip(scale, state)]
                while len(terms) > 1:
                    terms = [a + b for a, b in zip(terms[::2], terms[1::2])]
                gbuf[pl.ds(i, 8, stride=span), :] = gate[i] * (terms[0] + direct * x)
                return state

            lax.fori_loop(0, span, emit, tuple(start), unroll=2)
            gsend[ct, :, gl * lanes : (gl + 1) * lanes] = gbuf[...].astype(jnp.bfloat16)

        for n in range(len(others)):
            g_push(n, ct).start()
        gath[me, :, pl.ds(pl.multiple_of(ct * tile, tile), tile)] = gsend[
            ct, pl.ds(pl.multiple_of(s * rows, rows), rows)
        ]

    for k in range(4):
        ow_copy(k).wait()

    for step in range(4):
        z = nearest_first(t, step)
        for ds in range(2):
            source = z * 2 + lax.rem(s + ds, 2)
            if (step, ds) != (0, 0):
                for ct in range(2):
                    part = gath.at[source, :, pl.ds(ct * tile, tile)]
                    pltpu.make_async_copy(part, part, g_recv.at[source, ct]).wait()
            depth = pl.ds(pl.multiple_of(source * half, half), half)
            part = jnp.dot(gath[source], ow[depth, :], preferred_element_type=jnp.float32)
            if (step, ds) == (0, 0):
                acc[...] = part
            elif (step, ds) == (3, 1):
                out[...] = (acc[...] + part).astype(out.dtype)
            else:
                acc[...] += part

    for dt in (1, 2, 3):
        f_push(dt).wait_send()

    @pl.when(home != s)
    def _():
        f_push(0).wait_send()

    for ct in range(2):
        for j in range(3):
            p_push(ct, j).wait_send()
        for n in range(len(others)):
            g_push(n, ct).wait_send()


def fused_body(features, in_weight, short_taps, decay_rates, residues, skip_gain, out_weight):
    rows, deep = features.shape
    channels = in_weight.shape[2]
    half = channels // 2
    tile = half // 2
    lanes = tile // 2
    span = 2 * rows // 8
    rim = short_taps.shape[1] - 1
    f32, bf16 = jnp.float32, jnp.bfloat16
    dma = pltpu.SemaphoreType.DMA
    vmem = pl.BlockSpec(memory_space=pltpu.VMEM)
    hbm = pl.BlockSpec(memory_space=pl.ANY)
    return pl.pallas_call(
        fused_kernel,
        out_shape=jax.ShapeDtypeStruct((rows, channels), bf16),
        in_specs=[hbm, hbm, vmem, vmem, vmem, vmem, hbm],
        out_specs=vmem,
        scratch_shapes=[
            pltpu.VMEM((2, 2 * rows, deep), bf16),
            pltpu.VMEM((3, 2 * deep, channels), bf16),
            pltpu.VMEM((4 * channels, channels), bf16),
            pltpu.VMEM((2, 3, 2, 2 * rows, lanes), f32),
            pltpu.VMEM((2, 3, 2, 2 * rows, lanes), f32),
            pltpu.VMEM((2, 3, 2, 2 * rows, lanes), f32),
            pltpu.VMEM((3, span + rim, 8, lanes), f32),
            pltpu.VMEM((span, 8, lanes), f32),
            pltpu.VMEM((span, 8, lanes), f32),
            pltpu.VMEM((2 * rows, lanes), f32),
            pltpu.VMEM((2, 2 * rows, tile), bf16),
            pltpu.VMEM((8, rows, half), bf16),
            pltpu.VMEM((rows, channels), f32),
            dma((4,)),
            dma((2, 2)),
            dma((2, 3)),
            dma((4,)),
            dma((2, 3)),
            dma((2, 3)),
            dma((7, 2)),
            dma((8, 2)),
        ],
        compiler_params=pltpu.CompilerParams(
            collective_id=0, has_side_effects=True, vmem_limit_bytes=50 * 1024 * 1024
        ),
        cost_estimate=pl.CostEstimate(
            flops=2 * rows * 4 * channels * 4 * channels,
            bytes_accessed=10 * deep * channels * 2,
            transcendentals=0,
        ),
        name="mixer",
    )(
        features,
        jnp.transpose(in_weight, (1, 0, 2)),
        short_taps,
        decay_rates,
        residues,
        skip_gain[None, :],
        out_weight,
    )


def solution(mesh):
    in_specs = (
        P(("dp", "seq"), "tensor"),
        P("seq", None, "tensor"),
        P(None, None, "tensor"),
        P(None, "tensor"),
        P(None, "tensor"),
        P("tensor"),
        P(None, "tensor"),
    )
    out_specs = P(("dp", "seq"), "tensor")
    if mesh.shape["seq"] == 2 and mesh.shape["tensor"] == 4:
        return jax.shard_map(
            fused_body, mesh=mesh, in_specs=in_specs, out_specs=out_specs, check_vma=False
        )
    return jax.shard_map(body, mesh=mesh, in_specs=in_specs, out_specs=out_specs, check_vma=False)
```

```python
import functools

import jax
import jax.numpy as jnp
from jax import lax
from jax.experimental import pallas as pl
from jax.experimental.pallas import tpu as pltpu
from jax.sharding import PartitionSpec as P

MESH = pl.DeviceIdType.MESH

precise = lax.Precision.HIGHEST
block_len = 64


def passed_along(value, axis, steps):
    count = lax.axis_size(axis)
    leading, last = (max(0, -steps), min(count, count - steps))
    return lax.ppermute(value, axis, [(source, source + steps) for source in range(leading, last)])


def prefix_2(part, axis, combine, identity):
    place = lax.axis_index(axis)
    gathered = jax.tree.map(lambda a: lax.all_gather(a, axis), part)
    state = jax.tree.map(lambda a, e: jnp.zeros_like(a) + jnp.asarray(e, a.dtype), part, identity)

    def one(turn, state):
        return combine(
            state, jax.tree.map(lambda a: lax.dynamic_index_in_dim(a, turn, 0, False), gathered)
        )

    return lax.fori_loop(0, place, one, state)


def body(features, in_weight, short_taps, decay_rates, residues, skip_gain, out_weight):
    tok_rows = features.shape[0]
    channels = in_weight.shape[2]
    taps_count = short_taps.shape[1]
    whole_feats = lax.all_gather(features, "tensor", axis=1, tiled=True)
    piece = lax.all_gather(in_weight, "seq", axis=0, tiled=True)
    count = piece.shape[0]
    projected = jnp.dot(
        whole_feats, piece.reshape(count, 3 * channels), preferred_element_type=jnp.float32
    )
    projected = projected.astype(jnp.bfloat16).reshape(tok_rows, 3, channels)
    rim_rows = taps_count - 1
    earlier = passed_along(projected[tok_rows - rim_rows :], "seq", 1)
    extended = jnp.concatenate([earlier, projected], axis=0).astype(jnp.float32)
    short = jnp.zeros((tok_rows, 3, channels), jnp.float32)
    for offset_lag in range(taps_count):
        short = (
            short
            + short_taps[:, offset_lag, :][None]
            * extended[rim_rows - offset_lag : rim_rows - offset_lag + tok_rows]
        )
    product = short[:, 1, :] * short[:, 2, :]
    blocks = tok_rows // block_len
    pieces = product.reshape(blocks, block_len, channels)
    amplitude = residues * jnp.sqrt(2.0 * decay_rates)
    offsets = jnp.arange(block_len).astype(jnp.float32)
    falloff = jnp.exp(-decay_rates[:, None, :] * offsets[None, :, None])
    kernel = jnp.einsum("mc,mtc->tc", amplitude, falloff, precision=precise)
    lag_grid = jnp.arange(block_len)[:, None] - jnp.arange(block_len)[None, :]
    select = (lag_grid[:, :, None] == jnp.arange(block_len)[None, None, :]).astype(jnp.float32)
    toeplitz = jnp.einsum("tsk,kc->tsc", select, kernel, precision=precise)
    inner = jnp.einsum("tsc,bsc->btc", toeplitz, pieces, precision=precise)
    toward_end = jnp.exp(-decay_rates[:, None, :] * (block_len - offsets)[None, :, None])
    block_sums = jnp.einsum("msc,bsc->bmc", toward_end, pieces, precision=precise)
    block_index = jnp.arange(blocks).astype(jnp.float32)
    carry_over = jnp.exp(
        -decay_rates[None] * (block_len * (blocks - 1 - block_index))[:, None, None]
    )
    device_sum = jnp.sum(carry_over * block_sums, axis=0)
    device_decay = jnp.exp(-decay_rates * float(tok_rows))

    def combine(earlier_pair, later_pair):
        return (earlier_pair[0] * later_pair[0], later_pair[0] * earlier_pair[1] + later_pair[1])

    prefix = prefix_2(
        (device_decay, device_sum),
        "seq",
        combine,
        (jnp.ones_like(device_decay), jnp.zeros_like(device_sum)),
    )
    entering = prefix[1]
    step_decay = jnp.exp(-decay_rates * float(block_len))

    def advance(state, block_sum):
        return (step_decay * state + block_sum, state)

    final_state, starts = lax.scan(advance, entering, block_sums)
    outer = jnp.einsum("mic,bmc->bic", amplitude[:, None, :] * falloff, starts, precision=precise)
    conv = (inner + outer).reshape(tok_rows, channels)
    gated = (short[:, 0, :] * (conv + skip_gain[None, :] * product)).astype(jnp.bfloat16)
    mixed = jnp.dot(
        lax.all_gather(gated, "tensor", axis=1, tiled=True),
        out_weight,
        preferred_element_type=jnp.float32,
    )
    return mixed.astype(jnp.bfloat16)


def arrival_order(place, step):
    table = ((0, 1, 2, 3), (1, 3, 0, 2), (2, 0, 3, 1), (3, 2, 1, 0))
    found = jnp.int32(table[0][step])
    for at in range(1, 4):
        found = jnp.where(place == at, jnp.int32(table[at][step]), found)
    return found


def fused_kernel(
    feat, w_hbm, taps_hbm, decay_hbm, resid_hbm, skip_hbm, ow_hbm, out,
    f, w, ow, taps, decay, resid, skip, psend, precv, own, proj, prod, gate, rims, carry,
    gbuf, gsend, gath, acc,
    f_send, f_recv, fr_send, w_sem, ow_sem, c_sem, p_send, p_recv, g_send, g_recv, gr_send,
):
    rows, deep = feat.shape
    lanes = own.shape[-1]
    half = lanes * 4
    tile = half // 2
    span = rows // 8
    modes = decay.shape[0]
    taps_count = taps.shape[1]
    rim = taps_count - 1
    s = lax.axis_index("seq")
    t = lax.axis_index("tensor")
    me = t * 2 + s
    others = [(ds, dt) for dt in range(4) for ds in range(2) if (ds, dt) != (0, 0)]

    def device(ds, dt):
        return {"seq": lax.rem(s + ds, 2), "tensor": lax.rem(t + dt, 4)}

    near = jnp.where(t > 2 * s, 1, 0)
    mine = pl.ds(pl.multiple_of(s * half, half), half)

    def w_copy(step, j):
        r = near if step == 0 else 1 - near
        rng = pl.ds(pl.multiple_of(r * deep, deep), deep)
        return pltpu.make_async_copy(w_hbm.at[j, rng], w.at[j, rng], w_sem.at[step, j])

    def ow_copy(k):
        rng = pl.ds(k * deep, deep)
        return pltpu.make_async_copy(ow_hbm.at[rng], ow.at[rng], ow_sem.at[k])

    small = [
        pltpu.make_async_copy(taps_hbm.at[:, :, mine], taps, c_sem.at[0]),
        pltpu.make_async_copy(decay_hbm.at[:, mine], decay, c_sem.at[1]),
        pltpu.make_async_copy(resid_hbm.at[:, mine], resid, c_sem.at[2]),
        pltpu.make_async_copy(skip_hbm.at[:, mine], skip, c_sem.at[3]),
    ]

    barrier = pltpu.get_barrier_semaphore()
    for ds, dt in others:
        pl.semaphore_signal(barrier, inc=1, device_id=device(ds, dt), device_id_type=MESH)
    for step in range(2):
        for j in range(3):
            w_copy(step, j).start()
    for copy in small:
        copy.start()
    pl.semaphore_wait(barrier, len(others))

    home = t // 2
    slot = lax.rem(t, 2)

    def f_push(dt):
        return pltpu.make_async_remote_copy(
            src_ref=feat,
            dst_ref=f.at[slot, s],
            send_sem=f_send.at[dt],
            recv_sem=f_recv.at[slot, s],
            device_id={"seq": home, "tensor": lax.rem(t + dt, 4)},
            device_id_type=MESH,
        )

    def f_pushes():
        for dt in (2, 1, 3):
            @pl.when(f_goes(dt))
            def _(dt=dt):
                f_push(dt).start()

    def f_goes(dt):
        if dt == 2:
            return t < 4
        return (t != 0) if dt == 3 else (t != 3)

    @pl.when(home == s)
    def _():
        pltpu.make_async_copy(feat, f.at[slot, s], f_recv.at[slot, s]).start()

    @pl.when(home != s)
    def _():
        f_push(0).start()

    @pl.when(s == 0)
    def _():
        f_pushes()

    relays = jnp.where(s == 0, t == 2, t == 1)

    def f_relay(h):
        far = 1 - near
        return pltpu.make_async_remote_copy(
            src_ref=f.at[far, h],
            dst_ref=f.at[far, h],
            send_sem=fr_send.at[h],
            recv_sem=f_recv.at[far, h],
            device_id={"seq": s, "tensor": lax.rem(t + 1 + 2 * s, 4)},
            device_id_type=MESH,
        )

    def p_push(h, ct, j):
        return pltpu.make_async_remote_copy(
            src_ref=psend.at[h, ct, j],
            dst_ref=precv.at[h, ct, j],
            send_sem=p_send.at[h, ct, j],
            recv_sem=p_recv.at[h, ct, j],
            device_id=device(1, 0),
            device_id_type=MESH,
        )

    def in_projection(h):
        for step in range(2):
            r = near if step == 0 else 1 - near
            part = f.at[r, h]
            pltpu.make_async_copy(part, part, f_recv.at[r, h]).wait()
            if step == 1:

                @pl.when(relays)
                def _():
                    f_relay(h).start()

                if h == 0:

                    @pl.when(s == 1)
                    def _():
                        f_pushes()

            if h == 0:
                for j in range(3):
                    w_copy(step, j).wait()
            depth = pl.ds(pl.multiple_of(r * deep, deep), deep)
            for side in range(2):
                target = psend if side == 0 else own
                base = ((1 - s) if side == 0 else s) * half

                @pl.loop(0, 6)
                def _(idx, target=target, base=base, side=side, step=step, r=r, depth=depth):
                    ct, j = idx // 3, lax.rem(idx, 3)
                    columns = pl.ds(pl.multiple_of(base + ct * tile, tile), tile)
                    part = jnp.dot(
                        f[r, h], w[j, depth, columns], preferred_element_type=jnp.float32
                    )
                    for gl in range(2):
                        piece = part[:, gl * lanes : (gl + 1) * lanes]
                        if step == 0:
                            target[h, ct, j, gl] = piece
                        else:
                            target[h, ct, j, gl] += piece
                    if step == 1 and side == 0:
                        p_push(h, ct, j).start()

    first = lax.broadcasted_iota(jnp.int32, (8, lanes), 0)

    def later(value, by):
        return jnp.where(first >= by, pltpu.roll(value, by, 0), 0.0)

    def g_push(h, dt, ct):
        columns = pl.ds(pl.multiple_of(ct * tile, tile), tile)
        return pltpu.make_async_remote_copy(
            src_ref=gsend.at[h, :, columns],
            dst_ref=gath.at[me, :, columns],
            send_sem=g_send.at[h, dt, ct],
            recv_sem=g_recv.at[me, ct],
            device_id={"seq": h, "tensor": lax.rem(t + dt, 4)},
            device_id_type=MESH,
        )

    def g_goes(h, dt):
        return (s != h) if dt == 0 else f_goes(dt)

    def convolve(h, ct, gl):
        group = ct * 2 + gl
        columns = pl.ds(pl.multiple_of(group * lanes, lanes), lanes)

        @pl.loop(0, span, unroll=4)
        def _(i):
            at = pl.ds(i, 8, stride=span)
            for j in range(3):
                value = own.at[h, ct, j, gl][at, :] + precv.at[h, ct, j, gl][at, :]
                proj[j, rim + i] = value.astype(jnp.bfloat16).astype(jnp.float32)

        for j in range(3):
            for k in range(rim):
                last = proj[j, span + k]
                if h == 0:
                    proj[j, k] = later(last, 1)
                    rims[group, j, k] = pltpu.roll(last, 1, 0)
                else:
                    proj[j, k] = jnp.where(first >= 1, pltpu.roll(last, 1, 0), rims[group, j, k])

        tap = [
            [jnp.broadcast_to(taps[j, k : k + 1, columns], (8, lanes)) for k in range(taps_count)]
            for j in range(3)
        ]

        @pl.loop(0, span, unroll=2)
        def _(i):
            short = []
            for j in range(3):
                total = tap[j][0] * proj[j, rim + i]
                for k in range(1, taps_count):
                    total = total + tap[j][k] * proj[j, rim + i - k]
                short.append(total)
            gate[i] = short[0]
            prod[i] = short[1] * short[2]

        rate = [jnp.broadcast_to(decay[m : m + 1, columns], (8, lanes)) for m in range(modes)]
        fall = [jnp.exp(-v) for v in rate]

        def gather_state(i, state):
            x = prod[i]
            return tuple(a * v + x for a, v in zip(fall, state))

        zero = jnp.zeros((8, lanes), jnp.float32)
        state = lax.fori_loop(0, span, gather_state, (zero,) * modes, unroll=4)
        start = []
        for m in range(modes):
            jump = jnp.exp(-rate[m] * float(span))
            value = pltpu.roll(state[m], 1, 0)
            value = jnp.where(first >= 1, value, 0.0 if h == 0 else carry[group, m])
            for by in (1, 2, 4):
                value = value + jump * later(value, by)
                jump = jump * jump
            start.append(value)
        scale = [
            jnp.broadcast_to(resid[m : m + 1, columns], (8, lanes)) * jnp.sqrt(2.0 * rate[m])
            for m in range(modes)
        ]
        direct = jnp.broadcast_to(skip[:, columns], (8, lanes))

        def emit(i, state):
            x = prod[i]
            state = tuple(a * v + x for a, v in zip(fall, state))
            terms = [a * v for a, v in zip(scale, state)]
            while len(terms) > 1:
                terms = [a + b for a, b in zip(terms[::2], terms[1::2])]
            gbuf[pl.ds(i, 8, stride=span), :] = gate[i] * (terms[0] + direct * x)
            return state

        state = lax.fori_loop(0, span, emit, tuple(start), unroll=2)
        if h == 0:
            for m in range(modes):
                carry[group, m] = pltpu.roll(state[m], 1, 0)
        gsend[h, :, columns] = gbuf[...].astype(jnp.bfloat16)

    for h in range(2):
        in_projection(h)
        if h == 0:
            for k in range(4):
                ow_copy(k).start()
            for copy in small:
                copy.wait()

        @pl.loop(0, 2)
        def _(ct, h=h):
            for j in range(3):
                part = precv.at[h, ct, j]
                pltpu.make_async_copy(part, part, p_recv.at[h, ct, j]).wait()

            @pl.loop(0, 2)
            def _(gl):
                convolve(h, ct, gl)

            for dt in (2, 1, 3, 0):

                @pl.when(g_goes(h, dt))
                def _(dt=dt):
                    g_push(h, dt, ct).start()

        @pl.when(s == h)
        def _(h=h):
            gath[me] = gsend[h]

    for k in range(4):
        ow_copy(k).wait()

    middle = jnp.where(t == 1, True, t == 2)

    def g_relay(source, ds, ct):
        part = gath.at[source, :, pl.ds(ct * tile, tile)]
        return pltpu.make_async_remote_copy(
            src_ref=part,
            dst_ref=part,
            send_sem=gr_send.at[ds, ct],
            recv_sem=g_recv.at[source, ct],
            device_id={"seq": s, "tensor": jnp.where(t == 1, 0, 3)},
            device_id_type=MESH,
        )

    for step in range(4):
        z = arrival_order(t, step)
        for ds in range(2):
            source = z * 2 + lax.rem(s + ds, 2)
            if (step, ds) != (0, 0):
                for ct in range(2):
                    part = gath.at[source, :, pl.ds(ct * tile, tile)]
                    pltpu.make_async_copy(part, part, g_recv.at[source, ct]).wait()
                    if step == 1:

                        @pl.when(middle)
                        def _(source=source, ds=ds, ct=ct):
                            g_relay(source, ds, ct).start()

            depth = pl.ds(pl.multiple_of(source * half, half), half)
            part = jnp.dot(gath[source], ow[depth, :], preferred_element_type=jnp.float32)
            if (step, ds) == (0, 0):
                acc[...] = part
            elif (step, ds) == (3, 1):
                out[...] = (acc[...] + part).astype(out.dtype)
            else:
                acc[...] += part

    for dt in (1, 2, 3):

        @pl.when(f_goes(dt))
        def _(dt=dt):
            f_push(dt).wait_send()

    @pl.when(home != s)
    def _():
        f_push(0).wait_send()

    @pl.when(relays)
    def _():
        for h in range(2):
            f_relay(h).wait_send()

    @pl.when(middle)
    def _():
        for ds in range(2):
            for ct in range(2):
                g_relay(arrival_order(t, 1) * 2 + lax.rem(s + ds, 2), ds, ct).wait_send()

    for h in range(2):
        for ct in range(2):
            for j in range(3):
                p_push(h, ct, j).wait_send()
            for dt in range(4):

                @pl.when(g_goes(h, dt))
                def _(h=h, ct=ct, dt=dt):
                    g_push(h, dt, ct).wait_send()


def fused_body(features, in_weight, short_taps, decay_rates, residues, skip_gain, out_weight):
    rows, deep = features.shape
    channels = in_weight.shape[2]
    half = channels // 2
    lanes = half // 4
    span = rows // 8
    modes = decay_rates.shape[0]
    taps_count = short_taps.shape[1]
    rim = taps_count - 1
    f32, bf16 = jnp.float32, jnp.bfloat16
    dma = pltpu.SemaphoreType.DMA
    vmem = pl.BlockSpec(memory_space=pltpu.VMEM)
    hbm = pl.BlockSpec(memory_space=pltpu.HBM)
    sums = pltpu.VMEM((2, 2, 3, 2, rows, lanes), f32)
    return pl.pallas_call(
        fused_kernel,
        out_shape=jax.ShapeDtypeStruct((rows, channels), bf16),
        in_specs=[hbm] * 7,
        out_specs=vmem,
        scratch_shapes=[
            pltpu.VMEM((2, 2, rows, deep), bf16),
            pltpu.VMEM((3, 2 * deep, channels), bf16),
            pltpu.VMEM((4 * channels, channels), bf16),
            pltpu.VMEM((3, taps_count, half), f32),
            pltpu.VMEM((modes, half), f32),
            pltpu.VMEM((modes, half), f32),
            pltpu.VMEM((1, half), f32),
            sums,
            sums,
            sums,
            pltpu.VMEM((3, span + rim, 8, lanes), f32),
            pltpu.VMEM((span, 8, lanes), f32),
            pltpu.VMEM((span, 8, lanes), f32),
            pltpu.VMEM((4, 3, rim, 8, lanes), f32),
            pltpu.VMEM((4, modes, 8, lanes), f32),
            pltpu.VMEM((rows, lanes), f32),
            pltpu.VMEM((2, rows, half), bf16),
            pltpu.VMEM((8, rows, half), bf16),
            pltpu.VMEM((rows, channels), f32),
            dma((4,)),
            dma((2, 2)),
            dma((2,)),
            dma((2, 3)),
            dma((4,)),
            dma((4,)),
            dma((2, 2, 3)),
            dma((2, 2, 3)),
            dma((2, 4, 2)),
            dma((8, 2)),
            dma((2, 2)),
        ],
        compiler_params=pltpu.CompilerParams(
            collective_id=0, has_side_effects=True, vmem_limit_bytes=50 * 1024 * 1024
        ),
        cost_estimate=pl.CostEstimate(
            flops=2 * rows * 4 * channels * 4 * channels,
            bytes_accessed=10 * deep * channels * 2,
            transcendentals=0,
        ),
        name="mixer",
    )(
        features,
        jnp.transpose(in_weight, (1, 0, 2)),
        short_taps,
        decay_rates,
        residues,
        skip_gain[None, :],
        out_weight,
    )


def solution(mesh):
    in_specs = (
        P(("dp", "seq"), "tensor"),
        P("seq", None, "tensor"),
        P(None, None, "tensor"),
        P(None, "tensor"),
        P(None, "tensor"),
        P("tensor"),
        P(None, "tensor"),
    )
    out_specs = P(("dp", "seq"), "tensor")
    if mesh.shape["seq"] == 2 and mesh.shape["tensor"] == 4:
        return jax.shard_map(
            fused_body, mesh=mesh, in_specs=in_specs, out_specs=out_specs, check_vma=False
        )
    return jax.shard_map(body, mesh=mesh, in_specs=in_specs, out_specs=out_specs, check_vma=False)
```

```python
import functools

import jax
import jax.numpy as jnp
from jax import lax
from jax.experimental import pallas as pl
from jax.experimental.pallas import tpu as pltpu
from jax.sharding import PartitionSpec as P

MESH = pl.DeviceIdType.MESH

precise = lax.Precision.HIGHEST
block_len = 64


def passed_along(value, axis, steps):
    count = lax.axis_size(axis)
    leading, last = (max(0, -steps), min(count, count - steps))
    return lax.ppermute(value, axis, [(source, source + steps) for source in range(leading, last)])


def prefix_2(part, axis, combine, identity):
    place = lax.axis_index(axis)
    gathered = jax.tree.map(lambda a: lax.all_gather(a, axis), part)
    state = jax.tree.map(lambda a, e: jnp.zeros_like(a) + jnp.asarray(e, a.dtype), part, identity)

    def one(turn, state):
        return combine(
            state, jax.tree.map(lambda a: lax.dynamic_index_in_dim(a, turn, 0, False), gathered)
        )

    return lax.fori_loop(0, place, one, state)


def body(features, in_weight, short_taps, decay_rates, residues, skip_gain, out_weight):
    tok_rows = features.shape[0]
    channels = in_weight.shape[2]
    taps_count = short_taps.shape[1]
    whole_feats = lax.all_gather(features, "tensor", axis=1, tiled=True)
    piece = lax.all_gather(in_weight, "seq", axis=0, tiled=True)
    count = piece.shape[0]
    projected = jnp.dot(
        whole_feats, piece.reshape(count, 3 * channels), preferred_element_type=jnp.float32
    )
    projected = projected.astype(jnp.bfloat16).reshape(tok_rows, 3, channels)
    rim_rows = taps_count - 1
    earlier = passed_along(projected[tok_rows - rim_rows :], "seq", 1)
    extended = jnp.concatenate([earlier, projected], axis=0).astype(jnp.float32)
    short = jnp.zeros((tok_rows, 3, channels), jnp.float32)
    for offset_lag in range(taps_count):
        short = (
            short
            + short_taps[:, offset_lag, :][None]
            * extended[rim_rows - offset_lag : rim_rows - offset_lag + tok_rows]
        )
    product = short[:, 1, :] * short[:, 2, :]
    blocks = tok_rows // block_len
    pieces = product.reshape(blocks, block_len, channels)
    amplitude = residues * jnp.sqrt(2.0 * decay_rates)
    offsets = jnp.arange(block_len).astype(jnp.float32)
    falloff = jnp.exp(-decay_rates[:, None, :] * offsets[None, :, None])
    kernel = jnp.einsum("mc,mtc->tc", amplitude, falloff, precision=precise)
    lag_grid = jnp.arange(block_len)[:, None] - jnp.arange(block_len)[None, :]
    select = (lag_grid[:, :, None] == jnp.arange(block_len)[None, None, :]).astype(jnp.float32)
    toeplitz = jnp.einsum("tsk,kc->tsc", select, kernel, precision=precise)
    inner = jnp.einsum("tsc,bsc->btc", toeplitz, pieces, precision=precise)
    toward_end = jnp.exp(-decay_rates[:, None, :] * (block_len - offsets)[None, :, None])
    block_sums = jnp.einsum("msc,bsc->bmc", toward_end, pieces, precision=precise)
    block_index = jnp.arange(blocks).astype(jnp.float32)
    carry_over = jnp.exp(
        -decay_rates[None] * (block_len * (blocks - 1 - block_index))[:, None, None]
    )
    device_sum = jnp.sum(carry_over * block_sums, axis=0)
    device_decay = jnp.exp(-decay_rates * float(tok_rows))

    def combine(earlier_pair, later_pair):
        return (earlier_pair[0] * later_pair[0], later_pair[0] * earlier_pair[1] + later_pair[1])

    prefix = prefix_2(
        (device_decay, device_sum),
        "seq",
        combine,
        (jnp.ones_like(device_decay), jnp.zeros_like(device_sum)),
    )
    entering = prefix[1]
    step_decay = jnp.exp(-decay_rates * float(block_len))

    def advance(state, block_sum):
        return (step_decay * state + block_sum, state)

    final_state, starts = lax.scan(advance, entering, block_sums)
    outer = jnp.einsum("mic,bmc->bic", amplitude[:, None, :] * falloff, starts, precision=precise)
    conv = (inner + outer).reshape(tok_rows, channels)
    gated = (short[:, 0, :] * (conv + skip_gain[None, :] * product)).astype(jnp.bfloat16)
    mixed = jnp.dot(
        lax.all_gather(gated, "tensor", axis=1, tiled=True),
        out_weight,
        preferred_element_type=jnp.float32,
    )
    return mixed.astype(jnp.bfloat16)


def arrival_order(place, step):
    table = ((0, 1, 2, 3), (1, 3, 0, 2), (2, 0, 3, 1), (3, 2, 1, 0))
    found = jnp.int32(table[0][step])
    for at in range(1, 4):
        found = jnp.where(place == at, jnp.int32(table[at][step]), found)
    return found


def fused_kernel(
    feat, w_hbm, taps_hbm, decay_hbm, resid_hbm, skip_hbm, ow_hbm, out,
    f, w, ow, taps, decay, resid, skip, plain, mixed_rows, tabs, psend, precv, own, proj, prod, gate,
    rims, carry, gbuf, gsend, gath, acc,
    f_send, f_recv, fr_send, w_sem, ow_sem, c_sem, p_send, p_recv, g_send, g_recv, gr_send,
):
    rows, deep = plain.shape
    lanes = own.shape[-1]
    half = lanes * 4
    tile = half // 2
    span = rows // 8
    modes = decay.shape[0]
    taps_count = taps.shape[1]
    rim = taps_count - 1
    s = lax.axis_index("seq")
    t = lax.axis_index("tensor")
    me = t * 2 + s
    others = [(ds, dt) for dt in range(4) for ds in range(2) if (ds, dt) != (0, 0)]

    def device(ds, dt):
        return {"seq": lax.rem(s + ds, 2), "tensor": lax.rem(t + dt, 4)}

    near = jnp.where(t > 2 * s, 1, 0)
    mine = pl.ds(pl.multiple_of(s * half, half), half)

    def w_copy(step, j):
        r = near if step == 0 else 1 - near
        rng = pl.ds(pl.multiple_of(r * deep, deep), deep)
        return pltpu.make_async_copy(w_hbm.at[j, rng], w.at[j, rng], w_sem.at[step, j])

    def ow_copy(k):
        rng = pl.ds(k * deep, deep)
        return pltpu.make_async_copy(ow_hbm.at[rng], ow.at[rng], ow_sem.at[k])

    small = [
        pltpu.make_async_copy(taps_hbm.at[:, :, mine], taps, c_sem.at[0]),
        pltpu.make_async_copy(decay_hbm.at[:, mine], decay, c_sem.at[1]),
        pltpu.make_async_copy(resid_hbm.at[:, mine], resid, c_sem.at[2]),
        pltpu.make_async_copy(skip_hbm.at[:, mine], skip, c_sem.at[3]),
    ]
    load = pltpu.make_async_copy(feat, plain, c_sem.at[4])
    load.start()

    barrier = pltpu.get_barrier_semaphore()
    for ds, dt in others:
        pl.semaphore_signal(barrier, inc=1, device_id=device(ds, dt), device_id_type=MESH)
    for step in range(2):
        for j in range(3):
            w_copy(step, j).start()
    for copy in small:
        copy.start()
    down = lax.broadcasted_iota(jnp.int32, (rows, rows), 0)
    across = lax.broadcasted_iota(jnp.int32, (rows, rows), 1)
    to_steps = jnp.where(across == lax.rem(down, 8) * span + lax.div(down, 8), 1.0, 0.0)
    to_tokens = jnp.where(down == lax.rem(across, 8) * span + lax.div(across, 8), 1.0, 0.0)
    to_steps, to_tokens = to_steps.astype(jnp.bfloat16), to_tokens.astype(jnp.bfloat16)
    load.wait()
    mixed_rows[...] = jnp.dot(
        to_steps, plain[...], preferred_element_type=jnp.float32
    ).astype(jnp.bfloat16)
    pl.semaphore_wait(barrier, len(others))

    home = t // 2
    slot = lax.rem(t, 2)

    def f_push(dt):
        return pltpu.make_async_remote_copy(
            src_ref=mixed_rows,
            dst_ref=f.at[slot, s],
            send_sem=f_send.at[dt],
            recv_sem=f_recv.at[slot, s],
            device_id={"seq": home, "tensor": lax.rem(t + dt, 4)},
            device_id_type=MESH,
        )

    def f_pushes():
        for dt in (2, 1, 3):
            @pl.when(f_goes(dt))
            def _(dt=dt):
                f_push(dt).start()

    def f_goes(dt):
        if dt == 2:
            return t < 4
        return (t != 0) if dt == 3 else (t != 3)

    @pl.when(home == s)
    def _():
        pltpu.make_async_copy(mixed_rows, f.at[slot, s], f_recv.at[slot, s]).start()

    @pl.when(home != s)
    def _():
        f_push(0).start()

    @pl.when(s == 0)
    def _():
        f_pushes()

    relays = jnp.where(s == 0, t == 2, t == 1)

    def f_relay(h):
        far = 1 - near
        return pltpu.make_async_remote_copy(
            src_ref=f.at[far, h],
            dst_ref=f.at[far, h],
            send_sem=fr_send.at[h],
            recv_sem=f_recv.at[far, h],
            device_id={"seq": s, "tensor": lax.rem(t + 1 + 2 * s, 4)},
            device_id_type=MESH,
        )

    def p_push(h, ct, j):
        return pltpu.make_async_remote_copy(
            src_ref=psend.at[h, ct, j],
            dst_ref=precv.at[h, ct, j],
            send_sem=p_send.at[h, ct, j],
            recv_sem=p_recv.at[h, ct, j],
            device_id=device(1, 0),
            device_id_type=MESH,
        )

    def in_projection(h):
        for step in range(2):
            r = near if step == 0 else 1 - near
            part = f.at[r, h]
            pltpu.make_async_copy(part, part, f_recv.at[r, h]).wait()
            if step == 1:

                @pl.when(relays)
                def _():
                    f_relay(h).start()

                if h == 0:

                    @pl.when(s == 1)
                    def _():
                        f_pushes()

            if h == 0:
                for j in range(3):
                    w_copy(step, j).wait()
            depth = pl.ds(pl.multiple_of(r * deep, deep), deep)
            for side in range(2):
                target = psend if side == 0 else own
                base = ((1 - s) if side == 0 else s) * half

                @pl.loop(0, 6)
                def _(idx, target=target, base=base, side=side, step=step, r=r, depth=depth):
                    ct, j = idx // 3, lax.rem(idx, 3)
                    columns = pl.ds(pl.multiple_of(base + ct * tile, tile), tile)
                    part = jnp.dot(
                        f[r, h], w[j, depth, columns], preferred_element_type=jnp.float32
                    )
                    for gl in range(2):
                        piece = part[:, gl * lanes : (gl + 1) * lanes]
                        if step == 0:
                            target[h, ct, j, gl] = piece
                        else:
                            target[h, ct, j, gl] += piece
                    if step == 1 and side == 0:
                        p_push(h, ct, j).start()

    first = lax.broadcasted_iota(jnp.int32, (8, lanes), 0)

    def later(value, by):
        return jnp.where(first >= by, pltpu.roll(value, by, 0), 0.0)

    def g_push(h, dt, ct):
        columns = pl.ds(pl.multiple_of(ct * tile, tile), tile)
        return pltpu.make_async_remote_copy(
            src_ref=gsend.at[h, :, columns],
            dst_ref=gath.at[me, :, columns],
            send_sem=g_send.at[h, dt, ct],
            recv_sem=g_recv.at[me, ct],
            device_id={"seq": h, "tensor": lax.rem(t + dt, 4)},
            device_id_type=MESH,
        )

    def g_goes(h, dt):
        return (s != h) if dt == 0 else f_goes(dt)

    def convolve(h, ct, gl):
        group = ct * 2 + gl
        columns = pl.ds(pl.multiple_of(group * lanes, lanes), lanes)
        short = []
        for j in range(3):
            value = own[h, ct, j, gl] + precv[h, ct, j, gl]
            proj[j, rim * 8 :] = value.astype(jnp.bfloat16).astype(jnp.float32)
            for k in range(rim):
                last = pltpu.roll(proj[j, (span + k) * 8 : (span + k + 1) * 8], 1, 0)
                if h == 0:
                    rims[group, j, k] = last
                    last = jnp.where(first >= 1, last, 0.0)
                else:
                    last = jnp.where(first >= 1, last, rims[group, j, k])
                proj[j, k * 8 : (k + 1) * 8] = last
            total = taps[j, 0:1, columns] * proj[j, rim * 8 :]
            for k in range(1, taps_count):
                total = total + taps[j, k : k + 1, columns] * proj[j, pl.ds((rim - k) * 8, rows)]
            short.append(total)
        gate[...] = short[0]
        prod[...] = short[1] * short[2]

        def row(q, m):
            return jnp.broadcast_to(tabs[q, m : m + 1, columns], (8, lanes))

        def step_at(i):
            return slice(i * 8, (i + 1) * 8)

        size = modes // 2
        for low in (0, size):
            few = range(low, low + size)
            fall = [row(0, m) for m in few]
            state = [prod[step_at(0)]] * size
            for i in range(1, span):
                x = prod[step_at(i)]
                state = [a * v + x for a, v in zip(fall, state)]
            start = []
            for m, v in zip(few, state):
                value = pltpu.roll(v, 1, 0)
                value = jnp.where(first >= 1, value, 0.0 if h == 0 else carry[group, m])
                for q, by in enumerate((1, 2, 4)):
                    value = value + row(1 + q, m) * later(value, by)
                start.append(value)
            scale = [row(4, m) for m in few]
            state = start
            for i in range(span):
                x = prod[step_at(i)]
                state = [a * v + x for a, v in zip(fall, state)]
                terms = [a * v for a, v in zip(scale, state)]
                while len(terms) > 1:
                    terms = [a + b for a, b in zip(terms[::2], terms[1::2])]
                if low == 0:
                    gbuf[step_at(i)] = terms[0]
                else:
                    gbuf[step_at(i)] += terms[0]
            if h == 0:
                for m, v in zip(few, state):
                    carry[group, m] = pltpu.roll(v, 1, 0)
        result = gate[...] * (gbuf[...] + skip[:, columns] * prod[...])
        gsend[h, :, columns] = result.astype(jnp.bfloat16)

    for copy in small:
        copy.wait()
    jump = jnp.exp(-decay[...] * float(span))
    tabs[0] = jnp.exp(-decay[...])
    tabs[1] = jump
    tabs[2] = jump * jump
    tabs[3] = (jump * jump) * (jump * jump)
    tabs[4] = resid[...] * jnp.sqrt(2.0 * decay[...])
    for k in range(4):
        ow_copy(k).start()

    for h in range(2):
        in_projection(h)

        @pl.loop(0, 2)
        def _(ct, h=h):
            for j in range(3):
                part = precv.at[h, ct, j]
                pltpu.make_async_copy(part, part, p_recv.at[h, ct, j]).wait()

            @pl.loop(0, 2)
            def _(gl):
                convolve(h, ct, gl)

            for dt in (2, 1, 3, 0):

                @pl.when(g_goes(h, dt))
                def _(dt=dt):
                    g_push(h, dt, ct).start()

        @pl.when(s == h)
        def _(h=h):
            gath[me] = gsend[h]

    for k in range(4):
        ow_copy(k).wait()

    middle = jnp.where(t == 1, True, t == 2)

    def g_relay(source, ds, ct):
        part = gath.at[source, :, pl.ds(ct * tile, tile)]
        return pltpu.make_async_remote_copy(
            src_ref=part,
            dst_ref=part,
            send_sem=gr_send.at[ds, ct],
            recv_sem=g_recv.at[source, ct],
            device_id={"seq": s, "tensor": jnp.where(t == 1, 0, 3)},
            device_id_type=MESH,
        )

    for step in range(4):
        z = arrival_order(t, step)
        for ds in range(2):
            source = z * 2 + lax.rem(s + ds, 2)
            if (step, ds) != (0, 0):
                for ct in range(2):
                    part = gath.at[source, :, pl.ds(ct * tile, tile)]
                    pltpu.make_async_copy(part, part, g_recv.at[source, ct]).wait()
                    if step == 1:

                        @pl.when(middle)
                        def _(source=source, ds=ds, ct=ct):
                            g_relay(source, ds, ct).start()

            depth = pl.ds(pl.multiple_of(source * half, half), half)
            part = jnp.dot(gath[source], ow[depth, :], preferred_element_type=jnp.float32)
            if (step, ds) == (0, 0):
                acc[...] = part
            elif (step, ds) == (3, 1):
                done = (acc[...] + part).astype(out.dtype)
                out[...] = jnp.dot(
                    to_tokens, done, preferred_element_type=jnp.float32
                ).astype(out.dtype)
            else:
                acc[...] += part

    for dt in (1, 2, 3):

        @pl.when(f_goes(dt))
        def _(dt=dt):
            f_push(dt).wait_send()

    @pl.when(home != s)
    def _():
        f_push(0).wait_send()

    @pl.when(relays)
    def _():
        for h in range(2):
            f_relay(h).wait_send()

    @pl.when(middle)
    def _():
        for ds in range(2):
            for ct in range(2):
                g_relay(arrival_order(t, 1) * 2 + lax.rem(s + ds, 2), ds, ct).wait_send()

    for h in range(2):
        for ct in range(2):
            for j in range(3):
                p_push(h, ct, j).wait_send()
            for dt in range(4):

                @pl.when(g_goes(h, dt))
                def _(h=h, ct=ct, dt=dt):
                    g_push(h, dt, ct).wait_send()


def fused_body(features, in_weight, short_taps, decay_rates, residues, skip_gain, out_weight):
    rows, deep = features.shape
    channels = in_weight.shape[2]
    half = channels // 2
    lanes = half // 4
    span = rows // 8
    modes = decay_rates.shape[0]
    taps_count = short_taps.shape[1]
    rim = taps_count - 1
    f32, bf16 = jnp.float32, jnp.bfloat16
    dma = pltpu.SemaphoreType.DMA
    vmem = pl.BlockSpec(memory_space=pltpu.VMEM)
    hbm = pl.BlockSpec(memory_space=pltpu.HBM)
    sums = pltpu.VMEM((2, 2, 3, 2, rows, lanes), f32)
    return pl.pallas_call(
        fused_kernel,
        out_shape=jax.ShapeDtypeStruct((rows, channels), bf16),
        in_specs=[hbm] * 7,
        out_specs=vmem,
        scratch_shapes=[
            pltpu.VMEM((2, 2, rows, deep), bf16),
            pltpu.VMEM((3, 2 * deep, channels), bf16),
            pltpu.VMEM((4 * channels, channels), bf16),
            pltpu.VMEM((3, taps_count, half), f32),
            pltpu.VMEM((modes, half), f32),
            pltpu.VMEM((modes, half), f32),
            pltpu.VMEM((1, half), f32),
            pltpu.VMEM((rows, deep), bf16),
            pltpu.VMEM((rows, deep), bf16),
            pltpu.VMEM((5, modes, half), f32),
            sums,
            sums,
            sums,
            pltpu.VMEM((3, rows + 8 * rim, lanes), f32),
            pltpu.VMEM((rows, lanes), f32),
            pltpu.VMEM((rows, lanes), f32),
            pltpu.VMEM((4, 3, rim, 8, lanes), f32),
            pltpu.VMEM((4, modes, 8, lanes), f32),
            pltpu.VMEM((rows, lanes), f32),
            pltpu.VMEM((2, rows, half), bf16),
            pltpu.VMEM((8, rows, half), bf16),
            pltpu.VMEM((rows, channels), f32),
            dma((4,)),
            dma((2, 2)),
            dma((2,)),
            dma((2, 3)),
            dma((4,)),
            dma((5,)),
            dma((2, 2, 3)),
            dma((2, 2, 3)),
            dma((2, 4, 2)),
            dma((8, 2)),
            dma((2, 2)),
        ],
        compiler_params=pltpu.CompilerParams(
            collective_id=0, has_side_effects=True, vmem_limit_bytes=60 * 1024 * 1024
        ),
        cost_estimate=pl.CostEstimate(
            flops=2 * rows * 4 * channels * 4 * channels,
            bytes_accessed=10 * deep * channels * 2,
            transcendentals=0,
        ),
        name="mixer",
    )(
        features,
        jnp.transpose(in_weight, (1, 0, 2)),
        short_taps,
        decay_rates,
        residues,
        skip_gain[None, :],
        out_weight,
    )


def solution(mesh):
    in_specs = (
        P(("dp", "seq"), "tensor"),
        P("seq", None, "tensor"),
        P(None, None, "tensor"),
        P(None, "tensor"),
        P(None, "tensor"),
        P("tensor"),
        P(None, "tensor"),
    )
    out_specs = P(("dp", "seq"), "tensor")
    if mesh.shape["seq"] == 2 and mesh.shape["tensor"] == 4:
        return jax.shard_map(
            fused_body, mesh=mesh, in_specs=in_specs, out_specs=out_specs, check_vma=False
        )
    return jax.shard_map(body, mesh=mesh, in_specs=in_specs, out_specs=out_specs, check_vma=False)
```

```python
import functools

import jax
import jax.numpy as jnp
from jax import lax
from jax.experimental import pallas as pl
from jax.experimental.pallas import tpu as pltpu
from jax.sharding import PartitionSpec as P

MESH = pl.DeviceIdType.MESH

precise = lax.Precision.HIGHEST
block_len = 64


def passed_along(value, axis, steps):
    count = lax.axis_size(axis)
    leading, last = (max(0, -steps), min(count, count - steps))
    return lax.ppermute(value, axis, [(source, source + steps) for source in range(leading, last)])


def prefix_2(part, axis, combine, identity):
    place = lax.axis_index(axis)
    gathered = jax.tree.map(lambda a: lax.all_gather(a, axis), part)
    state = jax.tree.map(lambda a, e: jnp.zeros_like(a) + jnp.asarray(e, a.dtype), part, identity)

    def one(turn, state):
        return combine(
            state, jax.tree.map(lambda a: lax.dynamic_index_in_dim(a, turn, 0, False), gathered)
        )

    return lax.fori_loop(0, place, one, state)


def body(features, in_weight, short_taps, decay_rates, residues, skip_gain, out_weight):
    tok_rows = features.shape[0]
    channels = in_weight.shape[2]
    taps_count = short_taps.shape[1]
    whole_feats = lax.all_gather(features, "tensor", axis=1, tiled=True)
    piece = lax.all_gather(in_weight, "seq", axis=0, tiled=True)
    count = piece.shape[0]
    projected = jnp.dot(
        whole_feats, piece.reshape(count, 3 * channels), preferred_element_type=jnp.float32
    )
    projected = projected.astype(jnp.bfloat16).reshape(tok_rows, 3, channels)
    rim_rows = taps_count - 1
    earlier = passed_along(projected[tok_rows - rim_rows :], "seq", 1)
    extended = jnp.concatenate([earlier, projected], axis=0).astype(jnp.float32)
    short = jnp.zeros((tok_rows, 3, channels), jnp.float32)
    for offset_lag in range(taps_count):
        short = (
            short
            + short_taps[:, offset_lag, :][None]
            * extended[rim_rows - offset_lag : rim_rows - offset_lag + tok_rows]
        )
    product = short[:, 1, :] * short[:, 2, :]
    blocks = tok_rows // block_len
    pieces = product.reshape(blocks, block_len, channels)
    amplitude = residues * jnp.sqrt(2.0 * decay_rates)
    offsets = jnp.arange(block_len).astype(jnp.float32)
    falloff = jnp.exp(-decay_rates[:, None, :] * offsets[None, :, None])
    kernel = jnp.einsum("mc,mtc->tc", amplitude, falloff, precision=precise)
    lag_grid = jnp.arange(block_len)[:, None] - jnp.arange(block_len)[None, :]
    select = (lag_grid[:, :, None] == jnp.arange(block_len)[None, None, :]).astype(jnp.float32)
    toeplitz = jnp.einsum("tsk,kc->tsc", select, kernel, precision=precise)
    inner = jnp.einsum("tsc,bsc->btc", toeplitz, pieces, precision=precise)
    toward_end = jnp.exp(-decay_rates[:, None, :] * (block_len - offsets)[None, :, None])
    block_sums = jnp.einsum("msc,bsc->bmc", toward_end, pieces, precision=precise)
    block_index = jnp.arange(blocks).astype(jnp.float32)
    carry_over = jnp.exp(
        -decay_rates[None] * (block_len * (blocks - 1 - block_index))[:, None, None]
    )
    device_sum = jnp.sum(carry_over * block_sums, axis=0)
    device_decay = jnp.exp(-decay_rates * float(tok_rows))

    def combine(earlier_pair, later_pair):
        return (earlier_pair[0] * later_pair[0], later_pair[0] * earlier_pair[1] + later_pair[1])

    prefix = prefix_2(
        (device_decay, device_sum),
        "seq",
        combine,
        (jnp.ones_like(device_decay), jnp.zeros_like(device_sum)),
    )
    entering = prefix[1]
    step_decay = jnp.exp(-decay_rates * float(block_len))

    def advance(state, block_sum):
        return (step_decay * state + block_sum, state)

    final_state, starts = lax.scan(advance, entering, block_sums)
    outer = jnp.einsum("mic,bmc->bic", amplitude[:, None, :] * falloff, starts, precision=precise)
    conv = (inner + outer).reshape(tok_rows, channels)
    gated = (short[:, 0, :] * (conv + skip_gain[None, :] * product)).astype(jnp.bfloat16)
    mixed = jnp.dot(
        lax.all_gather(gated, "tensor", axis=1, tiled=True),
        out_weight,
        preferred_element_type=jnp.float32,
    )
    return mixed.astype(jnp.bfloat16)


def arrival_order(place, step):
    table = ((0, 1, 2, 3), (1, 3, 0, 2), (2, 0, 3, 1), (3, 2, 1, 0))
    found = jnp.int32(table[0][step])
    for at in range(1, 4):
        found = jnp.where(place == at, jnp.int32(table[at][step]), found)
    return found


def fused_kernel(
    feat, w_hbm, taps_hbm, decay_hbm, resid_hbm, skip_hbm, ow_hbm, out,
    f, w, ow, taps, decay, resid, skip, plain, mixed_rows, tabs, psend, precv, own, proj, prod, gate,
    rims, carry, gbuf, gsend, gath, acc,
    f_send, f_recv, fr_send, w_sem, ow_sem, c_sem, p_send, p_recv, g_send, g_recv, gr_send,
):
    rows, deep = plain.shape
    lanes = own.shape[-1]
    half = lanes * 4
    tile = half // 2
    span = rows // 8
    modes = decay.shape[0]
    taps_count = taps.shape[1]
    rim = taps_count - 1
    s = lax.axis_index("seq")
    t = lax.axis_index("tensor")
    me = t * 2 + s
    others = [(ds, dt) for dt in range(4) for ds in range(2) if (ds, dt) != (0, 0)]

    def device(ds, dt):
        return {"seq": lax.rem(s + ds, 2), "tensor": lax.rem(t + dt, 4)}

    near = jnp.where(t > 2 * s, 1, 0)
    mine = pl.ds(pl.multiple_of(s * half, half), half)

    def w_copy(step, j):
        r = near if step == 0 else 1 - near
        rng = pl.ds(pl.multiple_of(r * deep, deep), deep)
        return pltpu.make_async_copy(w_hbm.at[j, rng], w.at[j, rng], w_sem.at[step, j])

    def ow_copy(k):
        rng = pl.ds(k * deep, deep)
        return pltpu.make_async_copy(ow_hbm.at[rng], ow.at[rng], ow_sem.at[k])

    small = [
        pltpu.make_async_copy(taps_hbm.at[:, :, mine], taps, c_sem.at[0]),
        pltpu.make_async_copy(decay_hbm.at[:, mine], decay, c_sem.at[1]),
        pltpu.make_async_copy(resid_hbm.at[:, mine], resid, c_sem.at[2]),
        pltpu.make_async_copy(skip_hbm.at[:, mine], skip, c_sem.at[3]),
    ]
    load = pltpu.make_async_copy(feat, plain, c_sem.at[4])
    load.start()

    barrier = pltpu.get_barrier_semaphore()
    for ds, dt in others:
        pl.semaphore_signal(barrier, inc=1, device_id=device(ds, dt), device_id_type=MESH)
    for step in range(2):
        for j in range(3):
            w_copy(step, j).start()
    for copy in small:
        copy.start()
    down = lax.broadcasted_iota(jnp.int32, (rows, rows), 0)
    across = lax.broadcasted_iota(jnp.int32, (rows, rows), 1)
    to_steps = jnp.where(across == lax.rem(down, 8) * span + lax.div(down, 8), 1.0, 0.0)
    to_tokens = jnp.where(down == lax.rem(across, 8) * span + lax.div(across, 8), 1.0, 0.0)
    to_steps, to_tokens = to_steps.astype(jnp.bfloat16), to_tokens.astype(jnp.bfloat16)
    load.wait()
    mixed_rows[...] = jnp.dot(
        to_steps, plain[...], preferred_element_type=jnp.float32
    ).astype(jnp.bfloat16)
    pl.semaphore_wait(barrier, len(others))

    home = t // 2
    slot = lax.rem(t, 2)
    along = jnp.where(s == 0, t, 3 - t)
    ahead = jnp.where(s == 0, 1, 3)

    def f_home():
        return pltpu.make_async_remote_copy(
            src_ref=mixed_rows,
            dst_ref=f.at[slot, s],
            send_sem=f_send,
            recv_sem=f_recv.at[slot, s],
            device_id=device(1, 0),
            device_id_type=MESH,
        )

    @pl.when(home == s)
    def _():
        pltpu.make_async_copy(mixed_rows, f.at[slot, s], f_recv.at[slot, s]).start()

    @pl.when(home != s)
    def _():
        f_home().start()

    def f_pass(h, step, back):
        r = near if step == 0 else 1 - near
        return pltpu.make_async_remote_copy(
            src_ref=f.at[r, h],
            dst_ref=f.at[r, h],
            send_sem=fr_send.at[h, step, back],
            recv_sem=f_recv.at[r, h],
            device_id={"seq": s, "tensor": lax.rem(t + (4 - ahead if back else ahead), 4)},
            device_id_type=MESH,
        )

    def f_passes(step, back):
        if step == 0:
            return along == 1 if back else along < 3
        return jnp.where(along == 1, True, along == 2)

    def f_take(h, step):
        r = near if step == 0 else 1 - near
        part = f.at[r, h]
        pltpu.make_async_copy(part, part, f_recv.at[r, h]).wait()
        for back in range(2 - step):

            @pl.when(f_passes(step, back))
            def _(back=back):
                f_pass(h, step, back).start()

    def p_push(h, ct, j):
        return pltpu.make_async_remote_copy(
            src_ref=psend.at[h, ct, j],
            dst_ref=precv.at[h, ct, j],
            send_sem=p_send.at[h, ct, j],
            recv_sem=p_recv.at[h, ct, j],
            device_id=device(1, 0),
            device_id_type=MESH,
        )

    def in_projection(h):
        for step in range(2):
            r = near if step == 0 else 1 - near
            if h == 0:
                f_take(0, step)
                if step == 1:

                    @pl.when(along < 2)
                    def _():
                        f_take(1, 0)

                for j in range(3):
                    w_copy(step, j).wait()
            elif step == 1:
                f_take(1, 1)
            depth = pl.ds(pl.multiple_of(r * deep, deep), deep)
            for side in range(2):
                target = psend if side == 0 else own
                base = ((1 - s) if side == 0 else s) * half

                @pl.loop(0, 3)
                def _(j, target=target, base=base, side=side, step=step, r=r, depth=depth):
                    columns = pl.ds(pl.multiple_of(base, half), half)
                    part = jnp.dot(
                        f[r, h], w[j, depth, columns], preferred_element_type=jnp.float32
                    )
                    for group in range(4):
                        ct, gl = divmod(group, 2)
                        piece = part[:, group * lanes : (group + 1) * lanes]
                        if step == 0:
                            target[h, ct, j, gl] = piece
                        else:
                            target[h, ct, j, gl] += piece
                    if step == 1 and side == 0:
                        for ct in range(2):
                            p_push(h, ct, j).start()

        if h == 0:

            @pl.when(along > 1)
            def _():
                f_take(1, 0)

    first = lax.broadcasted_iota(jnp.int32, (8, lanes), 0)

    def later(value, by):
        return jnp.where(first >= by, pltpu.roll(value, by, 0), 0.0)

    def g_push(h, dt, ct):
        columns = pl.ds(pl.multiple_of(ct * tile, tile), tile)
        return pltpu.make_async_remote_copy(
            src_ref=gsend.at[h, :, columns],
            dst_ref=gath.at[me, :, columns],
            send_sem=g_send.at[h, dt, ct],
            recv_sem=g_recv.at[me, ct],
            device_id={"seq": h, "tensor": lax.rem(t + dt, 4)},
            device_id_type=MESH,
        )

    def g_goes(h, dt):
        if dt == 0:
            return s != h
        if dt == 2:
            return t < 4
        return t < 4 if h == 0 else (t != 0) if dt == 3 else (t != 3)

    def convolve(h, ct, gl):
        group = ct * 2 + gl
        columns = pl.ds(pl.multiple_of(group * lanes, lanes), lanes)
        short = []
        for j in range(3):
            value = own[h, ct, j, gl] + precv[h, ct, j, gl]
            proj[j, rim * 8 :] = value.astype(jnp.bfloat16).astype(jnp.float32)
            for k in range(rim):
                last = pltpu.roll(proj[j, (span + k) * 8 : (span + k + 1) * 8], 1, 0)
                if h == 0:
                    rims[group, j, k] = last
                    last = jnp.where(first >= 1, last, 0.0)
                else:
                    last = jnp.where(first >= 1, last, rims[group, j, k])
                proj[j, k * 8 : (k + 1) * 8] = last
            total = taps[j, 0:1, columns] * proj[j, rim * 8 :]
            for k in range(1, taps_count):
                total = total + taps[j, k : k + 1, columns] * proj[j, pl.ds((rim - k) * 8, rows)]
            short.append(total)
        gate[...] = short[0]
        prod[...] = short[1] * short[2]

        def row(q, m):
            return jnp.broadcast_to(tabs[q, m : m + 1, columns], (8, lanes))

        def step_at(i):
            return slice(i * 8, (i + 1) * 8)

        size = modes // 2
        for low in (0, size):
            few = range(low, low + size)
            fall = [row(0, m) for m in few]
            state = [prod[step_at(0)]] * size
            for i in range(1, span):
                x = prod[step_at(i)]
                state = [a * v + x for a, v in zip(fall, state)]
            start = []
            for m, v in zip(few, state):
                value = pltpu.roll(v, 1, 0)
                value = jnp.where(first >= 1, value, 0.0 if h == 0 else carry[group, m])
                for q, by in enumerate((1, 2, 4)):
                    value = value + row(1 + q, m) * later(value, by)
                start.append(value)
            scale = [row(4, m) for m in few]
            state = start
            for i in range(span):
                x = prod[step_at(i)]
                state = [a * v + x for a, v in zip(fall, state)]
                terms = [a * v for a, v in zip(scale, state)]
                while len(terms) > 1:
                    terms = [a + b for a, b in zip(terms[::2], terms[1::2])]
                if low == 0:
                    gbuf[step_at(i)] = terms[0]
                else:
                    gbuf[step_at(i)] += terms[0]
            if h == 0:
                for m, v in zip(few, state):
                    carry[group, m] = pltpu.roll(v, 1, 0)
        result = gate[...] * (gbuf[...] + skip[:, columns] * prod[...])
        gsend[h, :, columns] = result.astype(jnp.bfloat16)

    for copy in small:
        copy.wait()
    jump = jnp.exp(-decay[...] * float(span))
    tabs[0] = jnp.exp(-decay[...])
    tabs[1] = jump
    tabs[2] = jump * jump
    tabs[3] = (jump * jump) * (jump * jump)
    tabs[4] = resid[...] * jnp.sqrt(2.0 * decay[...])
    for k in range(4):
        ow_copy(k).start()

    for h in range(2):
        in_projection(h)

        @pl.loop(0, 2)
        def _(ct, h=h):
            for j in range(3):
                part = precv.at[h, ct, j]
                pltpu.make_async_copy(part, part, p_recv.at[h, ct, j]).wait()

            @pl.loop(0, 2)
            def _(gl):
                convolve(h, ct, gl)

            for dt in (2, 1, 3, 0):

                @pl.when(g_goes(h, dt))
                def _(dt=dt):
                    g_push(h, dt, ct).start()

        @pl.when(s == h)
        def _(h=h):
            gath[me] = gsend[h]

    for k in range(4):
        ow_copy(k).wait()

    middle = jnp.where(s == 0, False, jnp.where(t == 1, True, t == 2))

    def g_relay(source, ds, ct):
        part = gath.at[source, :, pl.ds(ct * tile, tile)]
        return pltpu.make_async_remote_copy(
            src_ref=part,
            dst_ref=part,
            send_sem=gr_send.at[ds, ct],
            recv_sem=g_recv.at[source, ct],
            device_id={"seq": s, "tensor": jnp.where(t == 1, 0, 3)},
            device_id_type=MESH,
        )

    for step in range(4):
        z = arrival_order(t, step)
        for ds in range(2):
            source = z * 2 + lax.rem(s + ds, 2)
            if (step, ds) != (0, 0):
                for ct in range(2):
                    part = gath.at[source, :, pl.ds(ct * tile, tile)]
                    pltpu.make_async_copy(part, part, g_recv.at[source, ct]).wait()
                    if step == 1:

                        @pl.when(middle)
                        def _(source=source, ds=ds, ct=ct):
                            g_relay(source, ds, ct).start()

            depth = pl.ds(pl.multiple_of(source * half, half), half)
            part = jnp.dot(gath[source], ow[depth, :], preferred_element_type=jnp.float32)
            if (step, ds) == (0, 0):
                acc[...] = part
            elif (step, ds) == (3, 1):
                done = (acc[...] + part).astype(out.dtype)
                out[...] = jnp.dot(
                    to_tokens, done, preferred_element_type=jnp.float32
                ).astype(out.dtype)
            else:
                acc[...] += part

    @pl.when(home != s)
    def _():
        f_home().wait_send()

    for h in range(2):
        for step in range(2):
            for back in range(2 - step):

                @pl.when(f_passes(step, back))
                def _(h=h, step=step, back=back):
                    f_pass(h, step, back).wait_send()

    @pl.when(middle)
    def _():
        for ds in range(2):
            for ct in range(2):
                g_relay(arrival_order(t, 1) * 2 + lax.rem(s + ds, 2), ds, ct).wait_send()

    for h in range(2):
        for ct in range(2):
            for j in range(3):
                p_push(h, ct, j).wait_send()
            for dt in range(4):

                @pl.when(g_goes(h, dt))
                def _(h=h, ct=ct, dt=dt):
                    g_push(h, dt, ct).wait_send()


def fused_body(features, in_weight, short_taps, decay_rates, residues, skip_gain, out_weight):
    rows, deep = features.shape
    channels = in_weight.shape[2]
    half = channels // 2
    lanes = half // 4
    span = rows // 8
    modes = decay_rates.shape[0]
    taps_count = short_taps.shape[1]
    rim = taps_count - 1
    f32, bf16 = jnp.float32, jnp.bfloat16
    dma = pltpu.SemaphoreType.DMA
    vmem = pl.BlockSpec(memory_space=pltpu.VMEM)
    hbm = pl.BlockSpec(memory_space=pltpu.HBM)
    sums = pltpu.VMEM((2, 2, 3, 2, rows, lanes), f32)
    return pl.pallas_call(
        fused_kernel,
        out_shape=jax.ShapeDtypeStruct((rows, channels), bf16),
        in_specs=[hbm] * 7,
        out_specs=vmem,
        scratch_shapes=[
            pltpu.VMEM((2, 2, rows, deep), bf16),
            pltpu.VMEM((3, 2 * deep, channels), bf16),
            pltpu.VMEM((4 * channels, channels), bf16),
            pltpu.VMEM((3, taps_count, half), f32),
            pltpu.VMEM((modes, half), f32),
            pltpu.VMEM((modes, half), f32),
            pltpu.VMEM((1, half), f32),
            pltpu.VMEM((rows, deep), bf16),
            pltpu.VMEM((rows, deep), bf16),
            pltpu.VMEM((5, modes, half), f32),
            sums,
            sums,
            sums,
            pltpu.VMEM((3, rows + 8 * rim, lanes), f32),
            pltpu.VMEM((rows, lanes), f32),
            pltpu.VMEM((rows, lanes), f32),
            pltpu.VMEM((4, 3, rim, 8, lanes), f32),
            pltpu.VMEM((4, modes, 8, lanes), f32),
            pltpu.VMEM((rows, lanes), f32),
            pltpu.VMEM((2, rows, half), bf16),
            pltpu.VMEM((8, rows, half), bf16),
            pltpu.VMEM((rows, channels), f32),
            dma,
            dma((2, 2)),
            dma((2, 2, 2)),
            dma((2, 3)),
            dma((4,)),
            dma((5,)),
            dma((2, 2, 3)),
            dma((2, 2, 3)),
            dma((2, 4, 2)),
            dma((8, 2)),
            dma((2, 2)),
        ],
        compiler_params=pltpu.CompilerParams(
            collective_id=0, has_side_effects=True, vmem_limit_bytes=60 * 1024 * 1024
        ),
        cost_estimate=pl.CostEstimate(
            flops=2 * rows * 4 * channels * 4 * channels,
            bytes_accessed=10 * deep * channels * 2,
            transcendentals=0,
        ),
        name="mixer",
    )(
        features,
        jnp.transpose(in_weight, (1, 0, 2)),
        short_taps,
        decay_rates,
        residues,
        skip_gain[None, :],
        out_weight,
    )


def solution(mesh):
    in_specs = (
        P(("dp", "seq"), "tensor"),
        P("seq", None, "tensor"),
        P(None, None, "tensor"),
        P(None, "tensor"),
        P(None, "tensor"),
        P("tensor"),
        P(None, "tensor"),
    )
    out_specs = P(("dp", "seq"), "tensor")
    if mesh.shape["seq"] == 2 and mesh.shape["tensor"] == 4:
        return jax.shard_map(
            fused_body, mesh=mesh, in_specs=in_specs, out_specs=out_specs, check_vma=False
        )
    return jax.shard_map(body, mesh=mesh, in_specs=in_specs, out_specs=out_specs, check_vma=False)
```

```python
import functools

import jax
import jax.numpy as jnp
from jax import lax
from jax.experimental import pallas as pl
from jax.experimental.pallas import tpu as pltpu
from jax.sharding import PartitionSpec as P

MESH = pl.DeviceIdType.MESH

precise = lax.Precision.HIGHEST
block_len = 64


def passed_along(value, axis, steps):
    count = lax.axis_size(axis)
    leading, last = (max(0, -steps), min(count, count - steps))
    return lax.ppermute(value, axis, [(source, source + steps) for source in range(leading, last)])


def prefix_2(part, axis, combine, identity):
    place = lax.axis_index(axis)
    gathered = jax.tree.map(lambda a: lax.all_gather(a, axis), part)
    state = jax.tree.map(lambda a, e: jnp.zeros_like(a) + jnp.asarray(e, a.dtype), part, identity)

    def one(turn, state):
        return combine(
            state, jax.tree.map(lambda a: lax.dynamic_index_in_dim(a, turn, 0, False), gathered)
        )

    return lax.fori_loop(0, place, one, state)


def body(features, in_weight, short_taps, decay_rates, residues, skip_gain, out_weight):
    tok_rows = features.shape[0]
    channels = in_weight.shape[2]
    taps_count = short_taps.shape[1]
    whole_feats = lax.all_gather(features, "tensor", axis=1, tiled=True)
    piece = lax.all_gather(in_weight, "seq", axis=0, tiled=True)
    count = piece.shape[0]
    projected = jnp.dot(
        whole_feats, piece.reshape(count, 3 * channels), preferred_element_type=jnp.float32
    )
    projected = projected.astype(jnp.bfloat16).reshape(tok_rows, 3, channels)
    rim_rows = taps_count - 1
    earlier = passed_along(projected[tok_rows - rim_rows :], "seq", 1)
    extended = jnp.concatenate([earlier, projected], axis=0).astype(jnp.float32)
    short = jnp.zeros((tok_rows, 3, channels), jnp.float32)
    for offset_lag in range(taps_count):
        short = (
            short
            + short_taps[:, offset_lag, :][None]
            * extended[rim_rows - offset_lag : rim_rows - offset_lag + tok_rows]
        )
    product = short[:, 1, :] * short[:, 2, :]
    blocks = tok_rows // block_len
    pieces = product.reshape(blocks, block_len, channels)
    amplitude = residues * jnp.sqrt(2.0 * decay_rates)
    offsets = jnp.arange(block_len).astype(jnp.float32)
    falloff = jnp.exp(-decay_rates[:, None, :] * offsets[None, :, None])
    kernel = jnp.einsum("mc,mtc->tc", amplitude, falloff, precision=precise)
    lag_grid = jnp.arange(block_len)[:, None] - jnp.arange(block_len)[None, :]
    select = (lag_grid[:, :, None] == jnp.arange(block_len)[None, None, :]).astype(jnp.float32)
    toeplitz = jnp.einsum("tsk,kc->tsc", select, kernel, precision=precise)
    inner = jnp.einsum("tsc,bsc->btc", toeplitz, pieces, precision=precise)
    toward_end = jnp.exp(-decay_rates[:, None, :] * (block_len - offsets)[None, :, None])
    block_sums = jnp.einsum("msc,bsc->bmc", toward_end, pieces, precision=precise)
    block_index = jnp.arange(blocks).astype(jnp.float32)
    carry_over = jnp.exp(
        -decay_rates[None] * (block_len * (blocks - 1 - block_index))[:, None, None]
    )
    device_sum = jnp.sum(carry_over * block_sums, axis=0)
    device_decay = jnp.exp(-decay_rates * float(tok_rows))

    def combine(earlier_pair, later_pair):
        return (earlier_pair[0] * later_pair[0], later_pair[0] * earlier_pair[1] + later_pair[1])

    prefix = prefix_2(
        (device_decay, device_sum),
        "seq",
        combine,
        (jnp.ones_like(device_decay), jnp.zeros_like(device_sum)),
    )
    entering = prefix[1]
    step_decay = jnp.exp(-decay_rates * float(block_len))

    def advance(state, block_sum):
        return (step_decay * state + block_sum, state)

    final_state, starts = lax.scan(advance, entering, block_sums)
    outer = jnp.einsum("mic,bmc->bic", amplitude[:, None, :] * falloff, starts, precision=precise)
    conv = (inner + outer).reshape(tok_rows, channels)
    gated = (short[:, 0, :] * (conv + skip_gain[None, :] * product)).astype(jnp.bfloat16)
    mixed = jnp.dot(
        lax.all_gather(gated, "tensor", axis=1, tiled=True),
        out_weight,
        preferred_element_type=jnp.float32,
    )
    return mixed.astype(jnp.bfloat16)


def fused_kernel(
    feat, w_hbm, taps_hbm, decay_hbm, resid_hbm, skip_hbm, ow_hbm, out,
    f, w, ow, taps, decay, resid, skip, plain, mixed_rows, tabs, psend, precv, own, proj, prod, gate,
    rims, carry, gbuf, gsend, gath, acc,
    f_send, f_recv, fr_send, w_sem, ow_sem, c_sem, p_send, p_recv, g_send, g_recv, gr_send,
):
    rows, deep = plain.shape
    lanes = own.shape[-1]
    half = lanes * 4
    tile = half // 2
    span = rows // 8
    modes = decay.shape[0]
    taps_count = taps.shape[1]
    rim = taps_count - 1
    s = lax.axis_index("seq")
    t = lax.axis_index("tensor")
    me = t * 2 + s
    others = [(ds, dt) for dt in range(4) for ds in range(2) if (ds, dt) != (0, 0)]

    def device(ds, dt):
        return {"seq": lax.rem(s + ds, 2), "tensor": lax.rem(t + dt, 4)}

    near = jnp.where(t > 2 * s, 1, 0)
    mine = pl.ds(pl.multiple_of(s * half, half), half)

    def w_copy(step, j):
        r = near if step == 0 else 1 - near
        rng = pl.ds(pl.multiple_of(r * deep, deep), deep)
        return pltpu.make_async_copy(w_hbm.at[j, rng], w.at[j, rng], w_sem.at[step, j])

    def ow_copy(k):
        rng = pl.ds(k * deep, deep)
        return pltpu.make_async_copy(ow_hbm.at[rng], ow.at[rng], ow_sem.at[k])

    small = [
        pltpu.make_async_copy(taps_hbm.at[:, :, mine], taps, c_sem.at[0]),
        pltpu.make_async_copy(decay_hbm.at[:, mine], decay, c_sem.at[1]),
        pltpu.make_async_copy(resid_hbm.at[:, mine], resid, c_sem.at[2]),
        pltpu.make_async_copy(skip_hbm.at[:, mine], skip, c_sem.at[3]),
    ]
    load = pltpu.make_async_copy(feat, plain, c_sem.at[4])
    load.start()

    barrier = pltpu.get_barrier_semaphore()
    for ds, dt in others:
        pl.semaphore_signal(barrier, inc=1, device_id=device(ds, dt), device_id_type=MESH)
    for step in range(2):
        for j in range(3):
            w_copy(step, j).start()
    for copy in small:
        copy.start()
    down = lax.broadcasted_iota(jnp.int32, (rows, rows), 0)
    across = lax.broadcasted_iota(jnp.int32, (rows, rows), 1)
    to_steps = jnp.where(across == lax.rem(down, 8) * span + lax.div(down, 8), 1.0, 0.0)
    to_tokens = jnp.where(down == lax.rem(across, 8) * span + lax.div(across, 8), 1.0, 0.0)
    to_steps, to_tokens = to_steps.astype(jnp.bfloat16), to_tokens.astype(jnp.bfloat16)
    load.wait()
    mixed_rows[...] = jnp.dot(
        to_steps, plain[...], preferred_element_type=jnp.float32
    ).astype(jnp.bfloat16)
    pl.semaphore_wait(barrier, len(others))

    home = t // 2
    slot = lax.rem(t, 2)
    along = jnp.where(s == 0, t, 3 - t)
    ahead = jnp.where(s == 0, 1, 3)

    def f_home():
        return pltpu.make_async_remote_copy(
            src_ref=mixed_rows,
            dst_ref=f.at[slot, s],
            send_sem=f_send,
            recv_sem=f_recv.at[slot, s],
            device_id=device(1, 0),
            device_id_type=MESH,
        )

    @pl.when(home == s)
    def _():
        pltpu.make_async_copy(mixed_rows, f.at[slot, s], f_recv.at[slot, s]).start()

    @pl.when(home != s)
    def _():
        f_home().start()

    def f_pass(h, step, back):
        r = near if step == 0 else 1 - near
        return pltpu.make_async_remote_copy(
            src_ref=f.at[r, h],
            dst_ref=f.at[r, h],
            send_sem=fr_send.at[h, step, back],
            recv_sem=f_recv.at[r, h],
            device_id={"seq": s, "tensor": lax.rem(t + (4 - ahead if back else ahead), 4)},
            device_id_type=MESH,
        )

    def f_passes(step, back):
        if step == 0:
            return along == 1 if back else along < 3
        return jnp.where(along == 1, True, along == 2)

    def f_take(h, step):
        r = near if step == 0 else 1 - near
        part = f.at[r, h]
        pltpu.make_async_copy(part, part, f_recv.at[r, h]).wait()
        for back in range(2 - step):

            @pl.when(f_passes(step, back))
            def _(back=back):
                f_pass(h, step, back).start()

    def p_push(h, ct, j):
        return pltpu.make_async_remote_copy(
            src_ref=psend.at[h, ct, j],
            dst_ref=precv.at[h, ct, j],
            send_sem=p_send.at[h, ct, j],
            recv_sem=p_recv.at[h, ct, j],
            device_id=device(1, 0),
            device_id_type=MESH,
        )

    def in_projection(h):
        for step in range(2):
            r = near if step == 0 else 1 - near
            if h == 0:
                f_take(0, step)
                if step == 1:

                    @pl.when(along < 2)
                    def _():
                        f_take(1, 0)

                for j in range(3):
                    w_copy(step, j).wait()
            elif step == 0:

                @pl.when(along == 3)
                def _():
                    f_take(1, 0)

            else:

                @pl.when(jnp.where(along == 0, True, along == 3))
                def _():
                    f_take(1, 1)

            depth = pl.ds(pl.multiple_of(r * deep, deep), deep)
            for side in range(2):
                target = psend if side == 0 else own
                base = ((1 - s) if side == 0 else s) * half

                @pl.loop(0, 3)
                def _(j, target=target, base=base, side=side, step=step, r=r, depth=depth):
                    columns = pl.ds(pl.multiple_of(base, half), half)
                    part = jnp.dot(
                        f[r, h], w[j, depth, columns], preferred_element_type=jnp.float32
                    )
                    for group in range(4):
                        ct, gl = divmod(group, 2)
                        piece = part[:, group * lanes : (group + 1) * lanes]
                        if step == 0:
                            target[h, ct, j, gl] = piece
                        else:
                            target[h, ct, j, gl] += piece
                    if step == 1 and side == 0:
                        for ct in range(2):
                            p_push(h, ct, j).start()

        if h == 0:

            @pl.when(along == 2)
            def _():
                f_take(1, 0)

            @pl.when(f_passes(1, 0))
            def _():
                f_take(1, 1)

    first = lax.broadcasted_iota(jnp.int32, (8, lanes), 0)

    def later(value, by):
        return jnp.where(first >= by, pltpu.roll(value, by, 0), 0.0)

    def g_push(h, dt, ct):
        columns = pl.ds(pl.multiple_of(ct * tile, tile), tile)
        return pltpu.make_async_remote_copy(
            src_ref=gsend.at[h, :, columns],
            dst_ref=gath.at[me, :, columns],
            send_sem=g_send.at[h, dt, ct],
            recv_sem=g_recv.at[me, ct],
            device_id={"seq": h, "tensor": lax.rem(t + dt, 4)},
            device_id_type=MESH,
        )

    def g_goes(h, dt):
        if dt == 0:
            return s != h
        if h == 0 or dt == 2:
            return t < 4 * (1 - h)
        return (t != 0) if dt == 3 else (t != 3)

    def convolve(h, ct, gl):
        group = ct * 2 + gl
        columns = pl.ds(pl.multiple_of(group * lanes, lanes), lanes)
        short = []
        for j in range(3):
            value = own[h, ct, j, gl] + precv[h, ct, j, gl]
            proj[j, rim * 8 :] = value.astype(jnp.bfloat16).astype(jnp.float32)
            for k in range(rim):
                last = pltpu.roll(proj[j, (span + k) * 8 : (span + k + 1) * 8], 1, 0)
                if h == 0:
                    rims[group, j, k] = last
                    last = jnp.where(first >= 1, last, 0.0)
                else:
                    last = jnp.where(first >= 1, last, rims[group, j, k])
                proj[j, k * 8 : (k + 1) * 8] = last
            total = taps[j, 0:1, columns] * proj[j, rim * 8 :]
            for k in range(1, taps_count):
                total = total + taps[j, k : k + 1, columns] * proj[j, pl.ds((rim - k) * 8, rows)]
            short.append(total)
        gate[...] = short[0]
        prod[...] = short[1] * short[2]

        def row(q, m):
            return jnp.broadcast_to(tabs[q, m : m + 1, columns], (8, lanes))

        def step_at(i):
            return slice(i * 8, (i + 1) * 8)

        size = modes // 2
        for low in (0, size):
            few = range(low, low + size)
            fall = [row(0, m) for m in few]
            state = [prod[step_at(0)]] * size
            for i in range(1, span):
                x = prod[step_at(i)]
                state = [a * v + x for a, v in zip(fall, state)]
            start = []
            for m, v in zip(few, state):
                value = pltpu.roll(v, 1, 0)
                value = jnp.where(first >= 1, value, 0.0 if h == 0 else carry[group, m])
                for q, by in enumerate((1, 2, 4)):
                    value = value + row(1 + q, m) * later(value, by)
                start.append(value)
            scale = [row(4, m) for m in few]
            state = start
            for i in range(span):
                x = prod[step_at(i)]
                state = [a * v + x for a, v in zip(fall, state)]
                terms = [a * v for a, v in zip(scale, state)]
                while len(terms) > 1:
                    terms = [a + b for a, b in zip(terms[::2], terms[1::2])]
                if low == 0:
                    gbuf[step_at(i)] = terms[0]
                else:
                    gbuf[step_at(i)] += terms[0]
            if h == 0:
                for m, v in zip(few, state):
                    carry[group, m] = pltpu.roll(v, 1, 0)
        result = gate[...] * (gbuf[...] + skip[:, columns] * prod[...])
        gsend[h, :, columns] = result.astype(jnp.bfloat16)

    for copy in small:
        copy.wait()
    jump = jnp.exp(-decay[...] * float(span))
    tabs[0] = jnp.exp(-decay[...])
    tabs[1] = jump
    tabs[2] = jump * jump
    tabs[3] = (jump * jump) * (jump * jump)
    tabs[4] = resid[...] * jnp.sqrt(2.0 * decay[...])
    for k in range(4):
        ow_copy(k).start()

    for h in range(2):
        in_projection(h)

        @pl.loop(0, 2)
        def _(ct, h=h):
            for j in range(3):
                part = precv.at[h, ct, j]
                pltpu.make_async_copy(part, part, p_recv.at[h, ct, j]).wait()

            @pl.loop(0, 2)
            def _(gl):
                convolve(h, ct, gl)

            for dt in (2, 1, 3, 0):

                @pl.when(g_goes(h, dt))
                def _(dt=dt):
                    g_push(h, dt, ct).start()

        @pl.when(s == h)
        def _(h=h):
            gath[me] = gsend[h]

    for k in range(4):
        ow_copy(k).wait()

    def g_pass(source, ct, back):
        part = gath.at[source, :, pl.ds(ct * tile, tile)]
        return pltpu.make_async_remote_copy(
            src_ref=part,
            dst_ref=part,
            send_sem=gr_send.at[source, ct],
            recv_sem=g_recv.at[source, ct],
            device_id={"seq": s, "tensor": lax.rem(t + (3 if back else 1), 4)},
            device_id_type=MESH,
        )

    def g_passes(back):
        return jnp.where(s == 0, False, (t > 0) if back else (t < 3))

    def add_from(source):
        depth = pl.ds(pl.multiple_of(source * half, half), half)
        acc[...] += jnp.dot(gath[source], ow[depth, :], preferred_element_type=jnp.float32)

    def g_wait(source, ct):
        part = gath.at[source, :, pl.ds(ct * tile, tile)]
        pltpu.make_async_copy(part, part, g_recv.at[source, ct]).wait()

    steps = [(away, back) for away in (1, 2, 3) for back in range(2)]

    def has(away, back):
        return t + away < 4 if back else t >= away

    acc[...] = jnp.zeros_like(acc)
    add_from(me)
    for ct in range(2):
        g_wait(t * 2 + 1 - s, ct)
    add_from(t * 2 + 1 - s)
    for away, back in steps:

        @pl.when(has(away, back))
        def _(away=away, back=back):
            z = t + away if back else t - away
            for ct in range(2):
                for ds in range(2):
                    g_wait(z * 2 + ds, ct)

                    @pl.when(g_passes(back))
                    def _(ct=ct, ds=ds):
                        g_pass(z * 2 + ds, ct, back).start()

            for ds in range(2):
                add_from(z * 2 + ds)

    out[...] = jnp.dot(
        to_tokens, acc[...].astype(out.dtype), preferred_element_type=jnp.float32
    ).astype(out.dtype)

    for away, back in steps:

        @pl.when(jnp.where(has(away, back), g_passes(back), False))
        def _(away=away, back=back):
            z = t + away if back else t - away
            for ct in range(2):
                for ds in range(2):
                    g_pass(z * 2 + ds, ct, back).wait_send()

    @pl.when(home != s)
    def _():
        f_home().wait_send()

    for h in range(2):
        for step in range(2):
            for back in range(2 - step):

                @pl.when(f_passes(step, back))
                def _(h=h, step=step, back=back):
                    f_pass(h, step, back).wait_send()

    for h in range(2):
        for ct in range(2):
            for j in range(3):
                p_push(h, ct, j).wait_send()
            for dt in range(4):

                @pl.when(g_goes(h, dt))
                def _(h=h, ct=ct, dt=dt):
                    g_push(h, dt, ct).wait_send()


def fused_body(features, in_weight, short_taps, decay_rates, residues, skip_gain, out_weight):
    rows, deep = features.shape
    channels = in_weight.shape[2]
    half = channels // 2
    lanes = half // 4
    span = rows // 8
    modes = decay_rates.shape[0]
    taps_count = short_taps.shape[1]
    rim = taps_count - 1
    f32, bf16 = jnp.float32, jnp.bfloat16
    dma = pltpu.SemaphoreType.DMA
    vmem = pl.BlockSpec(memory_space=pltpu.VMEM)
    hbm = pl.BlockSpec(memory_space=pltpu.HBM)
    sums = pltpu.VMEM((2, 2, 3, 2, rows, lanes), f32)
    return pl.pallas_call(
        fused_kernel,
        out_shape=jax.ShapeDtypeStruct((rows, channels), bf16),
        in_specs=[hbm] * 7,
        out_specs=vmem,
        scratch_shapes=[
            pltpu.VMEM((2, 2, rows, deep), bf16),
            pltpu.VMEM((3, 2 * deep, channels), bf16),
            pltpu.VMEM((4 * channels, channels), bf16),
            pltpu.VMEM((3, taps_count, half), f32),
            pltpu.VMEM((modes, half), f32),
            pltpu.VMEM((modes, half), f32),
            pltpu.VMEM((1, half), f32),
            pltpu.VMEM((rows, deep), bf16),
            pltpu.VMEM((rows, deep), bf16),
            pltpu.VMEM((5, modes, half), f32),
            sums,
            sums,
            sums,
            pltpu.VMEM((3, rows + 8 * rim, lanes), f32),
            pltpu.VMEM((rows, lanes), f32),
            pltpu.VMEM((rows, lanes), f32),
            pltpu.VMEM((4, 3, rim, 8, lanes), f32),
            pltpu.VMEM((4, modes, 8, lanes), f32),
            pltpu.VMEM((rows, lanes), f32),
            pltpu.VMEM((2, rows, half), bf16),
            pltpu.VMEM((8, rows, half), bf16),
            pltpu.VMEM((rows, channels), f32),
            dma,
            dma((2, 2)),
            dma((2, 2, 2)),
            dma((2, 3)),
            dma((4,)),
            dma((5,)),
            dma((2, 2, 3)),
            dma((2, 2, 3)),
            dma((2, 4, 2)),
            dma((8, 2)),
            dma((8, 2)),
        ],
        compiler_params=pltpu.CompilerParams(
            collective_id=0, has_side_effects=True, vmem_limit_bytes=60 * 1024 * 1024
        ),
        cost_estimate=pl.CostEstimate(
            flops=2 * rows * 4 * channels * 4 * channels,
            bytes_accessed=10 * deep * channels * 2,
            transcendentals=0,
        ),
        name="mixer",
    )(
        features,
        jnp.transpose(in_weight, (1, 0, 2)),
        short_taps,
        decay_rates,
        residues,
        skip_gain[None, :],
        out_weight,
    )


def solution(mesh):
    in_specs = (
        P(("dp", "seq"), "tensor"),
        P("seq", None, "tensor"),
        P(None, None, "tensor"),
        P(None, "tensor"),
        P(None, "tensor"),
        P("tensor"),
        P(None, "tensor"),
    )
    out_specs = P(("dp", "seq"), "tensor")
    if mesh.shape["seq"] == 2 and mesh.shape["tensor"] == 4:
        return jax.shard_map(
            fused_body, mesh=mesh, in_specs=in_specs, out_specs=out_specs, check_vma=False
        )
    return jax.shard_map(body, mesh=mesh, in_specs=in_specs, out_specs=out_specs, check_vma=False)
```

```python
import functools

import jax
import jax.numpy as jnp
from jax import lax
from jax.experimental import pallas as pl
from jax.experimental.pallas import tpu as pltpu
from jax.sharding import PartitionSpec as P

MESH = pl.DeviceIdType.MESH

precise = lax.Precision.HIGHEST
block_len = 64


def passed_along(value, axis, steps):
    count = lax.axis_size(axis)
    leading, last = (max(0, -steps), min(count, count - steps))
    return lax.ppermute(value, axis, [(source, source + steps) for source in range(leading, last)])


def prefix_2(part, axis, combine, identity):
    place = lax.axis_index(axis)
    gathered = jax.tree.map(lambda a: lax.all_gather(a, axis), part)
    state = jax.tree.map(lambda a, e: jnp.zeros_like(a) + jnp.asarray(e, a.dtype), part, identity)

    def one(turn, state):
        return combine(
            state, jax.tree.map(lambda a: lax.dynamic_index_in_dim(a, turn, 0, False), gathered)
        )

    return lax.fori_loop(0, place, one, state)


def body(features, in_weight, short_taps, decay_rates, residues, skip_gain, out_weight):
    tok_rows = features.shape[0]
    channels = in_weight.shape[2]
    taps_count = short_taps.shape[1]
    whole_feats = lax.all_gather(features, "tensor", axis=1, tiled=True)
    piece = lax.all_gather(in_weight, "seq", axis=0, tiled=True)
    count = piece.shape[0]
    projected = jnp.dot(
        whole_feats, piece.reshape(count, 3 * channels), preferred_element_type=jnp.float32
    )
    projected = projected.astype(jnp.bfloat16).reshape(tok_rows, 3, channels)
    rim_rows = taps_count - 1
    earlier = passed_along(projected[tok_rows - rim_rows :], "seq", 1)
    extended = jnp.concatenate([earlier, projected], axis=0).astype(jnp.float32)
    short = jnp.zeros((tok_rows, 3, channels), jnp.float32)
    for offset_lag in range(taps_count):
        short = (
            short
            + short_taps[:, offset_lag, :][None]
            * extended[rim_rows - offset_lag : rim_rows - offset_lag + tok_rows]
        )
    product = short[:, 1, :] * short[:, 2, :]
    blocks = tok_rows // block_len
    pieces = product.reshape(blocks, block_len, channels)
    amplitude = residues * jnp.sqrt(2.0 * decay_rates)
    offsets = jnp.arange(block_len).astype(jnp.float32)
    falloff = jnp.exp(-decay_rates[:, None, :] * offsets[None, :, None])
    kernel = jnp.einsum("mc,mtc->tc", amplitude, falloff, precision=precise)
    lag_grid = jnp.arange(block_len)[:, None] - jnp.arange(block_len)[None, :]
    select = (lag_grid[:, :, None] == jnp.arange(block_len)[None, None, :]).astype(jnp.float32)
    toeplitz = jnp.einsum("tsk,kc->tsc", select, kernel, precision=precise)
    inner = jnp.einsum("tsc,bsc->btc", toeplitz, pieces, precision=precise)
    toward_end = jnp.exp(-decay_rates[:, None, :] * (block_len - offsets)[None, :, None])
    block_sums = jnp.einsum("msc,bsc->bmc", toward_end, pieces, precision=precise)
    block_index = jnp.arange(blocks).astype(jnp.float32)
    carry_over = jnp.exp(
        -decay_rates[None] * (block_len * (blocks - 1 - block_index))[:, None, None]
    )
    device_sum = jnp.sum(carry_over * block_sums, axis=0)
    device_decay = jnp.exp(-decay_rates * float(tok_rows))

    def combine(earlier_pair, later_pair):
        return (earlier_pair[0] * later_pair[0], later_pair[0] * earlier_pair[1] + later_pair[1])

    prefix = prefix_2(
        (device_decay, device_sum),
        "seq",
        combine,
        (jnp.ones_like(device_decay), jnp.zeros_like(device_sum)),
    )
    entering = prefix[1]
    step_decay = jnp.exp(-decay_rates * float(block_len))

    def advance(state, block_sum):
        return (step_decay * state + block_sum, state)

    final_state, starts = lax.scan(advance, entering, block_sums)
    outer = jnp.einsum("mic,bmc->bic", amplitude[:, None, :] * falloff, starts, precision=precise)
    conv = (inner + outer).reshape(tok_rows, channels)
    gated = (short[:, 0, :] * (conv + skip_gain[None, :] * product)).astype(jnp.bfloat16)
    mixed = jnp.dot(
        lax.all_gather(gated, "tensor", axis=1, tiled=True),
        out_weight,
        preferred_element_type=jnp.float32,
    )
    return mixed.astype(jnp.bfloat16)


def fused_kernel(
    feat, w_hbm, taps_hbm, decay_hbm, resid_hbm, skip_hbm, ow_hbm, out,
    f, w, ow, taps, decay, resid, skip, plain, mixed_rows, tabs, psend, precv, own, proj, prod, gate,
    rims, carry, gbuf, gsend, gath, acc,
    f_send, f_recv, fr_send, w_sem, ow_sem, c_sem, p_send, p_recv, g_send, g_recv, gr_send,
):
    rows, deep = plain.shape
    lanes = own.shape[-1]
    half = lanes * 4
    tile = half // 2
    span = rows // 8
    modes = decay.shape[0]
    taps_count = taps.shape[1]
    rim = taps_count - 1
    s = lax.axis_index("seq")
    t = lax.axis_index("tensor")
    me = t * 2 + s
    others = [(ds, dt) for dt in range(4) for ds in range(2) if (ds, dt) != (0, 0)]

    def device(ds, dt):
        return {"seq": lax.rem(s + ds, 2), "tensor": lax.rem(t + dt, 4)}

    near = jnp.where(t > 2 * s, 1, 0)
    mine = pl.ds(pl.multiple_of(s * half, half), half)

    def w_copy(step, j):
        r = near if step == 0 else 1 - near
        rng = pl.ds(pl.multiple_of(r * deep, deep), deep)
        return pltpu.make_async_copy(w_hbm.at[j, rng], w.at[j, rng], w_sem.at[step, j])

    def ow_copy(k):
        rng = pl.ds(k * deep, deep)
        return pltpu.make_async_copy(ow_hbm.at[rng], ow.at[rng], ow_sem.at[k])

    small = [
        pltpu.make_async_copy(taps_hbm.at[:, :, mine], taps, c_sem.at[0]),
        pltpu.make_async_copy(decay_hbm.at[:, mine], decay, c_sem.at[1]),
        pltpu.make_async_copy(resid_hbm.at[:, mine], resid, c_sem.at[2]),
        pltpu.make_async_copy(skip_hbm.at[:, mine], skip, c_sem.at[3]),
    ]
    load = pltpu.make_async_copy(feat, plain, c_sem.at[4])
    load.start()

    barrier = pltpu.get_barrier_semaphore()
    for ds, dt in others:
        pl.semaphore_signal(barrier, inc=1, device_id=device(ds, dt), device_id_type=MESH)
    for step in range(2):
        for j in range(3):
            w_copy(step, j).start()
    for copy in small:
        copy.start()
    down = lax.broadcasted_iota(jnp.int32, (rows, rows), 0)
    across = lax.broadcasted_iota(jnp.int32, (rows, rows), 1)
    to_steps = jnp.where(across == lax.rem(down, 8) * span + lax.div(down, 8), 1.0, 0.0)
    to_tokens = jnp.where(down == lax.rem(across, 8) * span + lax.div(across, 8), 1.0, 0.0)
    to_steps, to_tokens = to_steps.astype(jnp.bfloat16), to_tokens.astype(jnp.bfloat16)
    load.wait()
    mixed_rows[...] = jnp.dot(
        to_steps, plain[...], preferred_element_type=jnp.float32
    ).astype(jnp.bfloat16)
    pl.semaphore_wait(barrier, len(others))

    home = t // 2
    slot = lax.rem(t, 2)
    along = jnp.where(s == 0, t, 3 - t)
    ahead = jnp.where(s == 0, 1, 3)

    def f_home():
        return pltpu.make_async_remote_copy(
            src_ref=mixed_rows,
            dst_ref=f.at[slot, s],
            send_sem=f_send,
            recv_sem=f_recv.at[slot, s],
            device_id=device(1, 0),
            device_id_type=MESH,
        )

    @pl.when(home == s)
    def _():
        pltpu.make_async_copy(mixed_rows, f.at[slot, s], f_recv.at[slot, s]).start()

    @pl.when(home != s)
    def _():
        f_home().start()

    def f_pass(h, step, back):
        r = near if step == 0 else 1 - near
        return pltpu.make_async_remote_copy(
            src_ref=f.at[r, h],
            dst_ref=f.at[r, h],
            send_sem=fr_send.at[h, step, back],
            recv_sem=f_recv.at[r, h],
            device_id={"seq": s, "tensor": lax.rem(t + (4 - ahead if back else ahead), 4)},
            device_id_type=MESH,
        )

    def f_passes(step, back):
        if step == 0:
            return along == 1 if back else along < 3
        return jnp.where(along == 1, True, along == 2)

    def f_take(h, step):
        r = near if step == 0 else 1 - near
        part = f.at[r, h]
        pltpu.make_async_copy(part, part, f_recv.at[r, h]).wait()
        for back in range(2 - step):

            @pl.when(f_passes(step, back))
            def _(back=back):
                f_pass(h, step, back).start()

    def p_push(h, ct, j):
        return pltpu.make_async_remote_copy(
            src_ref=psend.at[h, ct, j],
            dst_ref=precv.at[h, ct, j],
            send_sem=p_send.at[h, ct, j],
            recv_sem=p_recv.at[h, ct, j],
            device_id=device(1, 0),
            device_id_type=MESH,
        )

    def in_projection(h):
        for step in range(2):
            r = near if step == 0 else 1 - near
            if h == 0:
                f_take(0, step)
                if step == 1:

                    @pl.when(along < 2)
                    def _():
                        f_take(1, 0)

                for j in range(3):
                    w_copy(step, j).wait()
            elif step == 0:

                @pl.when(along == 3)
                def _():
                    f_take(1, 0)

            else:

                @pl.when(jnp.where(along == 0, True, along == 3))
                def _():
                    f_take(1, 1)

            depth = pl.ds(pl.multiple_of(r * deep, deep), deep)
            for side in range(2):
                target = psend if side == 0 else own
                base = ((1 - s) if side == 0 else s) * half

                @pl.loop(0, 3)
                def _(j, target=target, base=base, side=side, step=step, r=r, depth=depth):
                    columns = pl.ds(pl.multiple_of(base, half), half)
                    part = jnp.dot(
                        f[r, h], w[j, depth, columns], preferred_element_type=jnp.float32
                    )
                    for group in range(4):
                        ct, gl = divmod(group, 2)
                        piece = part[:, group * lanes : (group + 1) * lanes]
                        if step == 0:
                            target[h, ct, j, gl] = piece
                        else:
                            target[h, ct, j, gl] += piece
                    if step == 1 and side == 0:
                        for ct in range(2):
                            p_push(h, ct, j).start()

        if h == 0:

            @pl.when(along == 2)
            def _():
                f_take(1, 0)

            @pl.when(f_passes(1, 0))
            def _():
                f_take(1, 1)

    first = lax.broadcasted_iota(jnp.int32, (8, lanes), 0)

    def later(value, by):
        return jnp.where(first >= by, pltpu.roll(value, by, 0), 0.0)

    def g_push(h, dt, ct):
        return pltpu.make_async_remote_copy(
            src_ref=gsend.at[h, ct],
            dst_ref=gath.at[me, ct],
            send_sem=g_send.at[h, dt, ct],
            recv_sem=g_recv.at[me, ct],
            device_id={"seq": h, "tensor": lax.rem(t + dt, 4)},
            device_id_type=MESH,
        )

    def g_goes(h, dt):
        if dt == 0:
            return s != h
        if h == 0 or dt == 2:
            return t < 4 * (1 - h)
        return (t != 0) if dt == 3 else (t != 3)

    def convolve(h, ct, gl):
        group = ct * 2 + gl
        columns = pl.ds(pl.multiple_of(group * lanes, lanes), lanes)
        short = []
        for j in range(3):
            value = own[h, ct, j, gl] + precv[h, ct, j, gl]
            proj[j, rim * 8 :] = value.astype(jnp.bfloat16).astype(jnp.float32)
            for k in range(rim):
                last = pltpu.roll(proj[j, (span + k) * 8 : (span + k + 1) * 8], 1, 0)
                if h == 0:
                    rims[group, j, k] = last
                    last = jnp.where(first >= 1, last, 0.0)
                else:
                    last = jnp.where(first >= 1, last, rims[group, j, k])
                proj[j, k * 8 : (k + 1) * 8] = last
            total = taps[j, 0:1, columns] * proj[j, rim * 8 :]
            for k in range(1, taps_count):
                total = total + taps[j, k : k + 1, columns] * proj[j, pl.ds((rim - k) * 8, rows)]
            short.append(total)
        gate[...] = short[0]
        prod[...] = short[1] * short[2]

        def row(q, m):
            return jnp.broadcast_to(tabs[q, m : m + 1, columns], (8, lanes))

        def step_at(i):
            return slice(i * 8, (i + 1) * 8)

        size = modes // 2
        for low in (0, size):
            few = range(low, low + size)
            fall = [row(0, m) for m in few]
            state = [prod[step_at(0)]] * size
            for i in range(1, span):
                x = prod[step_at(i)]
                state = [a * v + x for a, v in zip(fall, state)]
            start = []
            for m, v in zip(few, state):
                value = pltpu.roll(v, 1, 0)
                value = jnp.where(first >= 1, value, 0.0 if h == 0 else carry[group, m])
                for q, by in enumerate((1, 2, 4)):
                    value = value + row(1 + q, m) * later(value, by)
                start.append(value)
            scale = [row(4, m) for m in few]
            state = start
            for i in range(span):
                x = prod[step_at(i)]
                state = [a * v + x for a, v in zip(fall, state)]
                terms = [a * v for a, v in zip(scale, state)]
                while len(terms) > 1:
                    terms = [a + b for a, b in zip(terms[::2], terms[1::2])]
                if low == 0:
                    gbuf[step_at(i)] = terms[0]
                else:
                    gbuf[step_at(i)] += terms[0]
            if h == 0:
                for m, v in zip(few, state):
                    carry[group, m] = pltpu.roll(v, 1, 0)
        result = gate[...] * (gbuf[...] + skip[:, columns] * prod[...])
        part = pl.ds(pl.multiple_of(gl * lanes, lanes), lanes)
        gsend[h, ct, :, part] = result.astype(jnp.bfloat16)

    for copy in small:
        copy.wait()
    jump = jnp.exp(-decay[...] * float(span))
    tabs[0] = jnp.exp(-decay[...])
    tabs[1] = jump
    tabs[2] = jump * jump
    tabs[3] = (jump * jump) * (jump * jump)
    tabs[4] = resid[...] * jnp.sqrt(2.0 * decay[...])
    for k in range(4):
        ow_copy(k).start()

    for h in range(2):
        in_projection(h)

        @pl.loop(0, 2)
        def _(ct, h=h):
            for j in range(3):
                part = precv.at[h, ct, j]
                pltpu.make_async_copy(part, part, p_recv.at[h, ct, j]).wait()

            @pl.loop(0, 2)
            def _(gl):
                convolve(h, ct, gl)

            for dt in (2, 1, 3, 0):

                @pl.when(g_goes(h, dt))
                def _(dt=dt):
                    g_push(h, dt, ct).start()

        @pl.when(s == h)
        def _(h=h):
            gath[me] = gsend[h]

    for k in range(4):
        ow_copy(k).wait()

    def g_pass(source, ct, back):
        part = gath.at[source, ct]
        return pltpu.make_async_remote_copy(
            src_ref=part,
            dst_ref=part,
            send_sem=gr_send.at[source, ct],
            recv_sem=g_recv.at[source, ct],
            device_id={"seq": s, "tensor": lax.rem(t + jnp.where(back == 1, 3, 1), 4)},
            device_id_type=MESH,
        )

    def g_passes(back):
        return jnp.where(s == 0, False, jnp.where(back == 1, t > 0, t < 3))

    def add_from(source):
        total = acc[...]
        for ct in range(2):
            depth = pl.ds(pl.multiple_of(source * half + ct * tile, tile), tile)
            total += jnp.dot(gath[source, ct], ow[depth, :], preferred_element_type=jnp.float32)
        acc[...] = total

    def g_wait(source, ct):
        part = gath.at[source, ct]
        pltpu.make_async_copy(part, part, g_recv.at[source, ct]).wait()

    inner = jnp.where(t < 2, 1, 0)
    steps = [(away, turn) for away in (1, 2, 3) for turn in range(2)]

    def has(away, back):
        return jnp.where(back == 1, t + away < 4, t >= away)

    acc[...] = jnp.zeros_like(acc)
    add_from(me)
    for ct in range(2):
        g_wait(t * 2 + 1 - s, ct)
    add_from(t * 2 + 1 - s)
    for away, turn in steps:
        back = inner if turn == 0 else 1 - inner

        @pl.when(has(away, back))
        def _(away=away, back=back):
            z = jnp.where(back == 1, t + away, t - away)
            for ct in range(2):
                for ds in range(2):
                    g_wait(z * 2 + ds, ct)

                    @pl.when(g_passes(back))
                    def _(ct=ct, ds=ds):
                        g_pass(z * 2 + ds, ct, back).start()

            for ds in range(2):
                add_from(z * 2 + ds)

    out[...] = jnp.dot(
        to_tokens, acc[...].astype(out.dtype), preferred_element_type=jnp.float32
    ).astype(out.dtype)

    for away, turn in steps:
        back = inner if turn == 0 else 1 - inner

        @pl.when(jnp.where(has(away, back), g_passes(back), False))
        def _(away=away, back=back):
            z = jnp.where(back == 1, t + away, t - away)
            for ct in range(2):
                for ds in range(2):
                    g_pass(z * 2 + ds, ct, back).wait_send()

    @pl.when(home != s)
    def _():
        f_home().wait_send()

    for h in range(2):
        for step in range(2):
            for back in range(2 - step):

                @pl.when(f_passes(step, back))
                def _(h=h, step=step, back=back):
                    f_pass(h, step, back).wait_send()

    for h in range(2):
        for ct in range(2):
            for j in range(3):
                p_push(h, ct, j).wait_send()
            for dt in range(4):

                @pl.when(g_goes(h, dt))
                def _(h=h, ct=ct, dt=dt):
                    g_push(h, dt, ct).wait_send()


def fused_body(features, in_weight, short_taps, decay_rates, residues, skip_gain, out_weight):
    rows, deep = features.shape
    channels = in_weight.shape[2]
    half = channels // 2
    lanes = half // 4
    span = rows // 8
    modes = decay_rates.shape[0]
    taps_count = short_taps.shape[1]
    rim = taps_count - 1
    f32, bf16 = jnp.float32, jnp.bfloat16
    dma = pltpu.SemaphoreType.DMA
    vmem = pl.BlockSpec(memory_space=pltpu.VMEM)
    hbm = pl.BlockSpec(memory_space=pltpu.HBM)
    sums = pltpu.VMEM((2, 2, 3, 2, rows, lanes), f32)
    return pl.pallas_call(
        fused_kernel,
        out_shape=jax.ShapeDtypeStruct((rows, channels), bf16),
        in_specs=[hbm] * 7,
        out_specs=vmem,
        scratch_shapes=[
            pltpu.VMEM((2, 2, rows, deep), bf16),
            pltpu.VMEM((3, 2 * deep, channels), bf16),
            pltpu.VMEM((4 * channels, channels), bf16),
            pltpu.VMEM((3, taps_count, half), f32),
            pltpu.VMEM((modes, half), f32),
            pltpu.VMEM((modes, half), f32),
            pltpu.VMEM((1, half), f32),
            pltpu.VMEM((rows, deep), bf16),
            pltpu.VMEM((rows, deep), bf16),
            pltpu.VMEM((5, modes, half), f32),
            sums,
            sums,
            sums,
            pltpu.VMEM((3, rows + 8 * rim, lanes), f32),
            pltpu.VMEM((rows, lanes), f32),
            pltpu.VMEM((rows, lanes), f32),
            pltpu.VMEM((4, 3, rim, 8, lanes), f32),
            pltpu.VMEM((4, modes, 8, lanes), f32),
            pltpu.VMEM((rows, lanes), f32),
            pltpu.VMEM((2, 2, rows, half // 2), bf16),
            pltpu.VMEM((8, 2, rows, half // 2), bf16),
            pltpu.VMEM((rows, channels), f32),
            dma,
            dma((2, 2)),
            dma((2, 2, 2)),
            dma((2, 3)),
            dma((4,)),
            dma((5,)),
            dma((2, 2, 3)),
            dma((2, 2, 3)),
            dma((2, 4, 2)),
            dma((8, 2)),
            dma((8, 2)),
        ],
        compiler_params=pltpu.CompilerParams(
            collective_id=0, has_side_effects=True, vmem_limit_bytes=60 * 1024 * 1024
        ),
        cost_estimate=pl.CostEstimate(
            flops=2 * rows * 4 * channels * 4 * channels,
            bytes_accessed=10 * deep * channels * 2,
            transcendentals=0,
        ),
        name="mixer",
    )(
        features,
        jnp.transpose(in_weight, (1, 0, 2)),
        short_taps,
        decay_rates,
        residues,
        skip_gain[None, :],
        out_weight,
    )


def solution(mesh):
    in_specs = (
        P(("dp", "seq"), "tensor"),
        P("seq", None, "tensor"),
        P(None, None, "tensor"),
        P(None, "tensor"),
        P(None, "tensor"),
        P("tensor"),
        P(None, "tensor"),
    )
    out_specs = P(("dp", "seq"), "tensor")
    if mesh.shape["seq"] == 2 and mesh.shape["tensor"] == 4:
        return jax.shard_map(
            fused_body, mesh=mesh, in_specs=in_specs, out_specs=out_specs, check_vma=False
        )
    return jax.shard_map(body, mesh=mesh, in_specs=in_specs, out_specs=out_specs, check_vma=False)
```

```python
import functools

import jax
import jax.numpy as jnp
from jax import lax
from jax.experimental import pallas as pl
from jax.experimental.pallas import tpu as pltpu
from jax.sharding import PartitionSpec as P

MESH = pl.DeviceIdType.MESH

precise = lax.Precision.HIGHEST
block_len = 64


def passed_along(value, axis, steps):
    count = lax.axis_size(axis)
    leading, last = (max(0, -steps), min(count, count - steps))
    return lax.ppermute(value, axis, [(source, source + steps) for source in range(leading, last)])


def prefix_2(part, axis, combine, identity):
    place = lax.axis_index(axis)
    gathered = jax.tree.map(lambda a: lax.all_gather(a, axis), part)
    state = jax.tree.map(lambda a, e: jnp.zeros_like(a) + jnp.asarray(e, a.dtype), part, identity)

    def one(turn, state):
        return combine(
            state, jax.tree.map(lambda a: lax.dynamic_index_in_dim(a, turn, 0, False), gathered)
        )

    return lax.fori_loop(0, place, one, state)


def body(features, in_weight, short_taps, decay_rates, residues, skip_gain, out_weight):
    tok_rows = features.shape[0]
    channels = in_weight.shape[2]
    taps_count = short_taps.shape[1]
    whole_feats = lax.all_gather(features, "tensor", axis=1, tiled=True)
    piece = lax.all_gather(in_weight, "seq", axis=0, tiled=True)
    count = piece.shape[0]
    projected = jnp.dot(
        whole_feats, piece.reshape(count, 3 * channels), preferred_element_type=jnp.float32
    )
    projected = projected.astype(jnp.bfloat16).reshape(tok_rows, 3, channels)
    rim_rows = taps_count - 1
    earlier = passed_along(projected[tok_rows - rim_rows :], "seq", 1)
    extended = jnp.concatenate([earlier, projected], axis=0).astype(jnp.float32)
    short = jnp.zeros((tok_rows, 3, channels), jnp.float32)
    for offset_lag in range(taps_count):
        short = (
            short
            + short_taps[:, offset_lag, :][None]
            * extended[rim_rows - offset_lag : rim_rows - offset_lag + tok_rows]
        )
    product = short[:, 1, :] * short[:, 2, :]
    blocks = tok_rows // block_len
    pieces = product.reshape(blocks, block_len, channels)
    amplitude = residues * jnp.sqrt(2.0 * decay_rates)
    offsets = jnp.arange(block_len).astype(jnp.float32)
    falloff = jnp.exp(-decay_rates[:, None, :] * offsets[None, :, None])
    kernel = jnp.einsum("mc,mtc->tc", amplitude, falloff, precision=precise)
    lag_grid = jnp.arange(block_len)[:, None] - jnp.arange(block_len)[None, :]
    select = (lag_grid[:, :, None] == jnp.arange(block_len)[None, None, :]).astype(jnp.float32)
    toeplitz = jnp.einsum("tsk,kc->tsc", select, kernel, precision=precise)
    inner = jnp.einsum("tsc,bsc->btc", toeplitz, pieces, precision=precise)
    toward_end = jnp.exp(-decay_rates[:, None, :] * (block_len - offsets)[None, :, None])
    block_sums = jnp.einsum("msc,bsc->bmc", toward_end, pieces, precision=precise)
    block_index = jnp.arange(blocks).astype(jnp.float32)
    carry_over = jnp.exp(
        -decay_rates[None] * (block_len * (blocks - 1 - block_index))[:, None, None]
    )
    device_sum = jnp.sum(carry_over * block_sums, axis=0)
    device_decay = jnp.exp(-decay_rates * float(tok_rows))

    def combine(earlier_pair, later_pair):
        return (earlier_pair[0] * later_pair[0], later_pair[0] * earlier_pair[1] + later_pair[1])

    prefix = prefix_2(
        (device_decay, device_sum),
        "seq",
        combine,
        (jnp.ones_like(device_decay), jnp.zeros_like(device_sum)),
    )
    entering = prefix[1]
    step_decay = jnp.exp(-decay_rates * float(block_len))

    def advance(state, block_sum):
        return (step_decay * state + block_sum, state)

    final_state, starts = lax.scan(advance, entering, block_sums)
    outer = jnp.einsum("mic,bmc->bic", amplitude[:, None, :] * falloff, starts, precision=precise)
    conv = (inner + outer).reshape(tok_rows, channels)
    gated = (short[:, 0, :] * (conv + skip_gain[None, :] * product)).astype(jnp.bfloat16)
    mixed = jnp.dot(
        lax.all_gather(gated, "tensor", axis=1, tiled=True),
        out_weight,
        preferred_element_type=jnp.float32,
    )
    return mixed.astype(jnp.bfloat16)


def fused_kernel(
    feat, w_hbm, taps_hbm, decay_hbm, resid_hbm, skip_hbm, ow_hbm, out,
    f, w, ow, taps, decay, resid, skip, plain, mixed_rows, tabs, psend, precv, own, proj, prod, gate,
    rims, carry, gbuf, gsend, gath, acc,
    f_send, f_recv, fr_send, w_sem, ow_sem, c_sem, p_send, p_recv, g_send, g_recv, gr_send,
):
    rows, deep = plain.shape
    lanes = own.shape[-1]
    half = lanes * 4
    tile = half // 2
    span = rows // 8
    modes = decay.shape[0]
    taps_count = taps.shape[1]
    rim = taps_count - 1
    s = lax.axis_index("seq")
    t = lax.axis_index("tensor")
    me = t * 2 + s
    others = [(ds, dt) for dt in range(4) for ds in range(2) if (ds, dt) != (0, 0)]

    def device(ds, dt):
        return {"seq": lax.rem(s + ds, 2), "tensor": lax.rem(t + dt, 4)}

    near = jnp.where(t > 2 * s, 1, 0)
    mine = pl.ds(pl.multiple_of(s * half, half), half)

    def w_copy(step, j):
        r = near if step == 0 else 1 - near
        rng = pl.ds(pl.multiple_of(r * deep, deep), deep)
        return pltpu.make_async_copy(w_hbm.at[j, rng], w.at[j, rng], w_sem.at[step, j])

    def ow_copy(k):
        rng = pl.ds(k * deep, deep)
        return pltpu.make_async_copy(ow_hbm.at[rng], ow.at[rng], ow_sem.at[k])

    small = [
        pltpu.make_async_copy(taps_hbm.at[:, :, mine], taps, c_sem.at[0]),
        pltpu.make_async_copy(decay_hbm.at[:, mine], decay, c_sem.at[1]),
        pltpu.make_async_copy(resid_hbm.at[:, mine], resid, c_sem.at[2]),
        pltpu.make_async_copy(skip_hbm.at[:, mine], skip, c_sem.at[3]),
    ]
    load = pltpu.make_async_copy(feat, plain, c_sem.at[4])
    load.start()

    barrier = pltpu.get_barrier_semaphore()
    for ds, dt in others:
        pl.semaphore_signal(barrier, inc=1, device_id=device(ds, dt), device_id_type=MESH)
    for step in range(2):
        for j in range(3):
            w_copy(step, j).start()
    for copy in small:
        copy.start()
    down = lax.broadcasted_iota(jnp.int32, (rows, rows), 0)
    across = lax.broadcasted_iota(jnp.int32, (rows, rows), 1)
    to_steps = jnp.where(across == lax.rem(down, 8) * span + lax.div(down, 8), 1.0, 0.0)
    to_tokens = jnp.where(down == lax.rem(across, 8) * span + lax.div(across, 8), 1.0, 0.0)
    to_steps, to_tokens = to_steps.astype(jnp.bfloat16), to_tokens.astype(jnp.bfloat16)
    load.wait()
    mixed_rows[...] = jnp.dot(
        to_steps, plain[...], preferred_element_type=jnp.float32
    ).astype(jnp.bfloat16)
    pl.semaphore_wait(barrier, len(others))

    home = t // 2
    slot = lax.rem(t, 2)
    along = jnp.where(s == 0, t, 3 - t)
    ahead = jnp.where(s == 0, 1, 3)

    def f_home():
        return pltpu.make_async_remote_copy(
            src_ref=mixed_rows,
            dst_ref=f.at[slot, s],
            send_sem=f_send,
            recv_sem=f_recv.at[slot, s],
            device_id=device(1, 0),
            device_id_type=MESH,
        )

    @pl.when(home == s)
    def _():
        pltpu.make_async_copy(mixed_rows, f.at[slot, s], f_recv.at[slot, s]).start()

    @pl.when(home != s)
    def _():
        f_home().start()

    def f_pass(h, step, back):
        r = near if step == 0 else 1 - near
        return pltpu.make_async_remote_copy(
            src_ref=f.at[r, h],
            dst_ref=f.at[r, h],
            send_sem=fr_send.at[h, step, back],
            recv_sem=f_recv.at[r, h],
            device_id={"seq": s, "tensor": lax.rem(t + (4 - ahead if back else ahead), 4)},
            device_id_type=MESH,
        )

    def f_passes(step, back):
        if step == 0:
            return along == 1 if back else along < 3
        return jnp.where(along == 1, True, along == 2)

    def f_take(h, step):
        r = near if step == 0 else 1 - near
        part = f.at[r, h]
        pltpu.make_async_copy(part, part, f_recv.at[r, h]).wait()
        for back in range(2 - step):

            @pl.when(f_passes(step, back))
            def _(back=back):
                f_pass(h, step, back).start()

    def p_push(h, ct, j):
        return pltpu.make_async_remote_copy(
            src_ref=psend.at[h, ct, j],
            dst_ref=precv.at[h, ct, j],
            send_sem=p_send.at[h, ct, j],
            recv_sem=p_recv.at[h, ct, j],
            device_id=device(1, 0),
            device_id_type=MESH,
        )

    def in_projection(h):
        for step in range(2):
            r = near if step == 0 else 1 - near
            if h == 0:
                f_take(0, step)
                if step == 1:

                    @pl.when(along < 2)
                    def _():
                        f_take(1, 0)

                for j in range(3):
                    w_copy(step, j).wait()
            elif step == 0:

                @pl.when(along == 3)
                def _():
                    f_take(1, 0)

            else:

                @pl.when(jnp.where(along == 0, True, along == 3))
                def _():
                    f_take(1, 1)

            depth = pl.ds(pl.multiple_of(r * deep, deep), deep)
            for side in range(2):
                target = psend if side == 0 else own
                base = ((1 - s) if side == 0 else s) * half

                @pl.loop(0, 3)
                def _(j, target=target, base=base, side=side, step=step, r=r, depth=depth):
                    columns = pl.ds(pl.multiple_of(base, half), half)
                    part = jnp.dot(
                        f[r, h], w[j, depth, columns], preferred_element_type=jnp.float32
                    )
                    for group in range(4):
                        ct, gl = divmod(group, 2)
                        piece = part[:, group * lanes : (group + 1) * lanes]
                        if step == 0:
                            target[h, ct, j, gl] = piece
                        else:
                            target[h, ct, j, gl] += piece
                    if step == 1 and side == 0:
                        for ct in range(2):
                            p_push(h, ct, j).start()

        if h == 0:

            @pl.when(along == 2)
            def _():
                f_take(1, 0)

            @pl.when(f_passes(1, 0))
            def _():
                f_take(1, 1)

    first = lax.broadcasted_iota(jnp.int32, (8, lanes), 0)

    def later(value, by):
        return jnp.where(first >= by, pltpu.roll(value, by, 0), 0.0)

    def g_push(h, dt, ct):
        return pltpu.make_async_remote_copy(
            src_ref=gsend.at[h, ct],
            dst_ref=gath.at[me, ct],
            send_sem=g_send.at[h, dt, ct],
            recv_sem=g_recv.at[me, ct],
            device_id={"seq": h, "tensor": lax.rem(t + dt, 4)},
            device_id_type=MESH,
        )

    def g_goes(h, dt):
        if dt == 0:
            return s != h
        if h == 0 or dt == 2:
            return t < 4 * (1 - h)
        return (t != 0) if dt == 3 else (t != 3)

    def convolve(h, ct, gl):
        group = ct * 2 + gl
        columns = pl.ds(pl.multiple_of(group * lanes, lanes), lanes)
        short = []
        for j in range(3):
            value = own[h, ct, j, gl] + precv[h, ct, j, gl]
            proj[j, rim * 8 :] = value.astype(jnp.bfloat16).astype(jnp.float32)
            for k in range(rim):
                last = pltpu.roll(proj[j, (span + k) * 8 : (span + k + 1) * 8], 1, 0)
                if h == 0:
                    rims[group, j, k] = last
                    last = jnp.where(first >= 1, last, 0.0)
                else:
                    last = jnp.where(first >= 1, last, rims[group, j, k])
                proj[j, k * 8 : (k + 1) * 8] = last
            total = taps[j, 0:1, columns] * proj[j, rim * 8 :]
            for k in range(1, taps_count):
                total = total + taps[j, k : k + 1, columns] * proj[j, pl.ds((rim - k) * 8, rows)]
            short.append(total)
        gate[...] = short[0]
        prod[...] = short[1] * short[2]

        def row(q, m):
            return jnp.broadcast_to(tabs[q, m : m + 1, columns], (8, lanes))

        def step_at(i):
            return slice(i * 8, (i + 1) * 8)

        size = modes // 2
        for low in (0, size):
            few = range(low, low + size)
            fall = [row(0, m) for m in few]
            state = [prod[step_at(0)]] * size
            for i in range(1, span):
                x = prod[step_at(i)]
                state = [a * v + x for a, v in zip(fall, state)]
            start = []
            for m, v in zip(few, state):
                value = pltpu.roll(v, 1, 0)
                value = jnp.where(first >= 1, value, 0.0 if h == 0 else carry[group, m])
                for q, by in enumerate((1, 2, 4)):
                    value = value + row(1 + q, m) * later(value, by)
                start.append(value)
            scale = [row(4, m) for m in few]
            state = start
            for i in range(span):
                x = prod[step_at(i)]
                state = [a * v + x for a, v in zip(fall, state)]
                terms = [a * v for a, v in zip(scale, state)]
                while len(terms) > 1:
                    terms = [a + b for a, b in zip(terms[::2], terms[1::2])]
                if low == 0:
                    gbuf[step_at(i)] = terms[0]
                else:
                    gbuf[step_at(i)] += terms[0]
            if h == 0:
                for m, v in zip(few, state):
                    carry[group, m] = pltpu.roll(v, 1, 0)
        result = gate[...] * (gbuf[...] + skip[:, columns] * prod[...])
        part = pl.ds(pl.multiple_of(gl * lanes, lanes), lanes)
        gsend[h, ct, :, part] = result.astype(jnp.bfloat16)

    for copy in small:
        copy.wait()
    jump = jnp.exp(-decay[...] * float(span))
    tabs[0] = jnp.exp(-decay[...])
    tabs[1] = jump
    tabs[2] = jump * jump
    tabs[3] = (jump * jump) * (jump * jump)
    tabs[4] = resid[...] * jnp.sqrt(2.0 * decay[...])
    for k in range(4):
        ow_copy(k).start()

    def g_start(h, ct):
        for dt in (2, 1, 3, 0):

            @pl.when(g_goes(h, dt))
            def _(dt=dt):
                g_push(h, dt, ct).start()

    for h in range(2):
        in_projection(h)
        if h == 1:
            for ct in range(2):
                g_start(0, ct)

        @pl.loop(0, 2)
        def _(ct, h=h):
            for j in range(3):
                part = precv.at[h, ct, j]
                pltpu.make_async_copy(part, part, p_recv.at[h, ct, j]).wait()

            @pl.loop(0, 2)
            def _(gl):
                convolve(h, ct, gl)

            if h == 1:
                g_start(1, ct)

        @pl.when(s == h)
        def _(h=h):
            gath[me] = gsend[h]

    for k in range(4):
        ow_copy(k).wait()

    def g_pass(source, ct, back):
        part = gath.at[source, ct]
        return pltpu.make_async_remote_copy(
            src_ref=part,
            dst_ref=part,
            send_sem=gr_send.at[source, ct],
            recv_sem=g_recv.at[source, ct],
            device_id={"seq": s, "tensor": lax.rem(t + jnp.where(back == 1, 3, 1), 4)},
            device_id_type=MESH,
        )

    def g_passes(back):
        return jnp.where(s == 0, False, jnp.where(back == 1, t > 0, t < 3))

    def add_from(source):
        total = acc[...]
        for ct in range(2):
            depth = pl.ds(pl.multiple_of(source * half + ct * tile, tile), tile)
            total += jnp.dot(gath[source, ct], ow[depth, :], preferred_element_type=jnp.float32)
        acc[...] = total

    def g_wait(source, ct):
        part = gath.at[source, ct]
        pltpu.make_async_copy(part, part, g_recv.at[source, ct]).wait()

    inner = jnp.where(t < 2, 1, 0)
    steps = [(away, turn) for away in (1, 2, 3) for turn in range(2)]

    def has(away, back):
        return jnp.where(back == 1, t + away < 4, t >= away)

    acc[...] = jnp.zeros_like(acc)
    add_from(me)
    for ct in range(2):
        g_wait(t * 2 + 1 - s, ct)
    add_from(t * 2 + 1 - s)
    for away, turn in steps:
        back = inner if turn == 0 else 1 - inner

        @pl.when(has(away, back))
        def _(away=away, back=back):
            z = jnp.where(back == 1, t + away, t - away)
            for ct in range(2):
                for ds in range(2):
                    g_wait(z * 2 + ds, ct)

                    @pl.when(g_passes(back))
                    def _(ct=ct, ds=ds):
                        g_pass(z * 2 + ds, ct, back).start()

            for ds in range(2):
                add_from(z * 2 + ds)

    out[...] = jnp.dot(
        to_tokens, acc[...].astype(out.dtype), preferred_element_type=jnp.float32
    ).astype(out.dtype)

    for away, turn in steps:
        back = inner if turn == 0 else 1 - inner

        @pl.when(jnp.where(has(away, back), g_passes(back), False))
        def _(away=away, back=back):
            z = jnp.where(back == 1, t + away, t - away)
            for ct in range(2):
                for ds in range(2):
                    g_pass(z * 2 + ds, ct, back).wait_send()

    @pl.when(home != s)
    def _():
        f_home().wait_send()

    for h in range(2):
        for step in range(2):
            for back in range(2 - step):

                @pl.when(f_passes(step, back))
                def _(h=h, step=step, back=back):
                    f_pass(h, step, back).wait_send()

    for h in range(2):
        for ct in range(2):
            for j in range(3):
                p_push(h, ct, j).wait_send()
            for dt in range(4):

                @pl.when(g_goes(h, dt))
                def _(h=h, ct=ct, dt=dt):
                    g_push(h, dt, ct).wait_send()


def fused_body(features, in_weight, short_taps, decay_rates, residues, skip_gain, out_weight):
    rows, deep = features.shape
    channels = in_weight.shape[2]
    half = channels // 2
    lanes = half // 4
    span = rows // 8
    modes = decay_rates.shape[0]
    taps_count = short_taps.shape[1]
    rim = taps_count - 1
    f32, bf16 = jnp.float32, jnp.bfloat16
    dma = pltpu.SemaphoreType.DMA
    vmem = pl.BlockSpec(memory_space=pltpu.VMEM)
    hbm = pl.BlockSpec(memory_space=pltpu.HBM)
    sums = pltpu.VMEM((2, 2, 3, 2, rows, lanes), f32)
    return pl.pallas_call(
        fused_kernel,
        out_shape=jax.ShapeDtypeStruct((rows, channels), bf16),
        in_specs=[hbm] * 7,
        out_specs=vmem,
        scratch_shapes=[
            pltpu.VMEM((2, 2, rows, deep), bf16),
            pltpu.VMEM((3, 2 * deep, channels), bf16),
            pltpu.VMEM((4 * channels, channels), bf16),
            pltpu.VMEM((3, taps_count, half), f32),
            pltpu.VMEM((modes, half), f32),
            pltpu.VMEM((modes, half), f32),
            pltpu.VMEM((1, half), f32),
            pltpu.VMEM((rows, deep), bf16),
            pltpu.VMEM((rows, deep), bf16),
            pltpu.VMEM((5, modes, half), f32),
            sums,
            sums,
            sums,
            pltpu.VMEM((3, rows + 8 * rim, lanes), f32),
            pltpu.VMEM((rows, lanes), f32),
            pltpu.VMEM((rows, lanes), f32),
            pltpu.VMEM((4, 3, rim, 8, lanes), f32),
            pltpu.VMEM((4, modes, 8, lanes), f32),
            pltpu.VMEM((rows, lanes), f32),
            pltpu.VMEM((2, 2, rows, half // 2), bf16),
            pltpu.VMEM((8, 2, rows, half // 2), bf16),
            pltpu.VMEM((rows, channels), f32),
            dma,
            dma((2, 2)),
            dma((2, 2, 2)),
            dma((2, 3)),
            dma((4,)),
            dma((5,)),
            dma((2, 2, 3)),
            dma((2, 2, 3)),
            dma((2, 4, 2)),
            dma((8, 2)),
            dma((8, 2)),
        ],
        compiler_params=pltpu.CompilerParams(
            collective_id=0, has_side_effects=True, vmem_limit_bytes=60 * 1024 * 1024
        ),
        cost_estimate=pl.CostEstimate(
            flops=2 * rows * 4 * channels * 4 * channels,
            bytes_accessed=10 * deep * channels * 2,
            transcendentals=0,
        ),
        name="mixer",
    )(
        features,
        jnp.transpose(in_weight, (1, 0, 2)),
        short_taps,
        decay_rates,
        residues,
        skip_gain[None, :],
        out_weight,
    )


def solution(mesh):
    in_specs = (
        P(("dp", "seq"), "tensor"),
        P("seq", None, "tensor"),
        P(None, None, "tensor"),
        P(None, "tensor"),
        P(None, "tensor"),
        P("tensor"),
        P(None, "tensor"),
    )
    out_specs = P(("dp", "seq"), "tensor")
    if mesh.shape["seq"] == 2 and mesh.shape["tensor"] == 4:
        return jax.shard_map(
            fused_body, mesh=mesh, in_specs=in_specs, out_specs=out_specs, check_vma=False
        )
    return jax.shard_map(body, mesh=mesh, in_specs=in_specs, out_specs=out_specs, check_vma=False)
```
